256 devices in a mesh: dp: 16 (over x_hi, z), tensor: 16 (over x_lo, y, core).
Axes of the slice: x: 4 (x_hi: 2, x_lo: 2; x = x_hi * 2 + x_lo), y: 4, z: 8, core: 2. Of those that a mesh axis runs over, the one named last changes fastest.
Arguments:
- normed: bfloat16 [16384, 4096], P(('dp', 'tensor')), may hold values from -24 to 24
- out_grad: bfloat16 [16384, 4096], P(('dp', 'tensor')), may hold values from -0.046875 to 0.046875
- attn_out: bfloat16 [16384, 4096], P('dp', 'tensor'), may hold values from -6 to 6
- d_query: bfloat16 [16384, 4096], P('dp', 'tensor'), may hold values from -0.046875 to 0.046875
- d_keyvalue: bfloat16 [16384, 4096], P('dp', 'tensor'), may hold values from -0.046875 to 0.046875
- positions: int32 [16384], P('dp'), may hold values from 0 to 4095
- w_query: bfloat16 [4096, 4096], P(None, 'tensor'), may hold values from -8 to 8
- w_keyvalue: bfloat16 [4096, 2048], P(None, 'tensor'), may hold values from -8 to 8
Outputs:
- hidden_grad: bfloat16 [16384, 4096], P(('dp', 'tensor'))
- query_weight_grad: bfloat16 [4096, 4096], P('dp', 'tensor')
- keyvalue_weight_grad: bfloat16 [4096, 2048], P('dp', 'tensor')
- out_weight_grad: bfloat16 [4096, 4096], P('tensor', 'dp')
The draws below stay inside these ranges and needn't reach their ends.
All inputs are finite; a program needn't handle non-finite values.
Results may differ from the reference program's by a relative error of at most 0.023.
Values may be sent and summed in bfloat16 or wider, within the bound.
A program may use at most 128 MiB of HBM per device.

```python
import jax
import jax.numpy as jnp
from jax import lax

D = 4096
HD = 128
QH_DEV = 2
TOK_DEV = 64
QH = 32
KVH = 8
TOKENS = 16384
N_DP = 16
N_TENSOR = 16


def set_ends(values, own_key, smallest, largest):
    longest = values.shape.index(max(values.shape))
    spots = []
    for shift in (0, 1):
        where = [jax.random.randint(jax.random.fold_in(own_key, axis), (), 0, length) for axis, length in enumerate(values.shape)]
        where[longest] = (where[longest] + shift) % values.shape[longest]
        spots.append(tuple(where))
    return values.at[spots[0]].set(smallest).at[spots[1]].set(largest)


def with_spikes(entries, stream_key, source, target, parts, factor):
    def block_of(axis_at):
        return (jnp.arange(entries.shape[axis_at]) // (entries.shape[axis_at] // parts)).reshape((-1,) + (1,) * (entries.ndim - 1 - axis_at))

    one_side = jax.random.permutation(stream_key, parts)[block_of(target)]
    other_side = (block_of(target) + parts // 2) % parts
    return jnp.where((block_of(source) == one_side) | (block_of(source) == other_side), factor * entries, entries)


def levels(rng, dims, pieces, least, high):
    level, own = 1.0, jax.random.fold_in(rng, 6)
    for axis_at, blocks in pieces:
        draws = jnp.exp(jax.random.uniform(jax.random.fold_in(own, axis_at), (blocks,), jnp.float32, least / len(pieces), high / len(pieces)))
        level = level * jnp.repeat(draws, dims[axis_at] // blocks).reshape([-1 if axis == axis_at else 1 for axis in range(len(dims))])
    return level


def noise(stream_key, extent, width, most, shards=(), kind=jnp.bfloat16):
    entries = width * jax.random.normal(stream_key, extent, jnp.float32)
    if shards:
        entries = entries * levels(stream_key, extent, shards, -0.22, 0.18)
    return jnp.clip(entries, -most, most).astype(kind)


def noise_with(stream_key, dims, deviation, reach, cuts, heavy, held_as=jnp.bfloat16):
    entries = deviation * jax.random.normal(stream_key, dims, jnp.float32)
    if cuts:
        entries = entries * levels(stream_key, dims, cuts, -0.22, 0.18)
    return jnp.clip(with_spikes(entries, jax.random.fold_in(stream_key, 3), *heavy), -reach, reach).astype(held_as)


def setup_inputs(seed: int = 0) -> dict:
    key_list = jax.random.split(jax.random.key(seed), 9)
    normed = noise_with(key_list[0], (TOKENS, D), 1.0, 24.0, ((0, 256),), (0, 1, 256, 6.0))
    out_grad = noise(key_list[1], (TOKENS, D), ((TOK_DEV * N_TENSOR * N_DP) ** -0.5), 0.046875, ((0, 256),))
    attn_out = noise(key_list[2], (TOKENS, QH * HD), 1.0, 6.0, ((0, 16), (1, 16)))
    d_query = noise(key_list[3], (TOKENS, QH * HD), ((TOK_DEV * N_TENSOR * N_DP) ** -0.5), 0.046875, ((0, 16), (1, 16)))
    d_keyvalue = noise(key_list[4], (TOKENS, 4 * KVH * HD), ((TOK_DEV * N_TENSOR * N_DP) ** -0.5), 0.046875, ((0, 16), (1, 16)))
    positions = set_ends(jax.random.randint(key_list[5], (TOKENS,), 0, 4096), jax.random.fold_in(key_list[5], 1), 0, 4095).astype(jnp.int32)
    w_query = noise(key_list[6], (D, QH * HD), (((TOK_DEV * N_TENSOR * N_DP) / ((QH_DEV + 2) * HD * N_TENSOR)) ** 0.5), 8.0, ((1, 16),))
    w_keyvalue = noise(key_list[7], (D, 2 * KVH * HD), (((TOK_DEV * N_TENSOR * N_DP) / ((QH_DEV + 2) * HD * N_TENSOR)) ** 0.5), 8.0, ((1, 16),))
    return {"normed": normed, "out_grad": out_grad, "attn_out": attn_out, "d_query": d_query, "d_keyvalue": d_keyvalue, "positions": positions, "w_query": w_query, "w_keyvalue": w_keyvalue}


def rotary_tables(positions, head_dim):
    half_width = head_dim // 2
    inverse = jnp.power(jnp.float32(1000000.0), -(jnp.arange(half_width, dtype=jnp.float32) * 2.0 / head_dim))
    angles = positions.astype(jnp.float32)[:, None] * inverse[None, :]
    angles = jnp.concatenate([angles, angles], axis=1)
    return jnp.cos(angles), jnp.sin(angles)


def rotary_back(grad_vals, cosine, sine):
    half_width = grad_vals.shape[-1] // 2
    scaled = grad_vals * sine
    turned = jnp.concatenate([scaled[..., half_width:], -scaled[..., :half_width]], axis=-1)
    return grad_vals * cosine + turned


def contract(left, right, left_dim, right_dim):
    return lax.dot_general(left, right, (((left_dim,), (right_dim,)), ((), ())), preferred_element_type=jnp.float32)


def rounded(value):
    return lax.optimization_barrier(value.astype(jnp.bfloat16)).astype(jnp.float32)


def reference(normed, out_grad, attn_out, d_query, d_keyvalue, positions, w_query, w_keyvalue):
    cosine, sine = rotary_tables(positions, HD)
    cosine = cosine[:, None, :]
    sine = sine[:, None, :]
    query_grad = rotary_back(d_query.astype(jnp.float32).reshape(TOKENS, QH, HD), cosine, sine)
    query_grad = query_grad.reshape(TOKENS, QH * HD).astype(jnp.bfloat16)
    pairs = d_keyvalue.astype(jnp.float32).reshape(TOKENS, 2 * KVH, 2, HD)
    key_part = rotary_back(pairs[:, :, 0, :], cosine, sine)
    keyvalue_grad = jnp.stack([key_part, pairs[:, :, 1, :]], axis=2).reshape(TOKENS, 4 * KVH * HD).astype(jnp.bfloat16)

    query_groups = query_grad.reshape(TOKENS, N_TENSOR, QH_DEV * HD)
    kv_groups = keyvalue_grad.reshape(TOKENS, KVH, 2, 2, HD).transpose(0, 1, 3, 2, 4).reshape(TOKENS, N_TENSOR, 2 * HD)
    wq_groups = w_query.reshape(D, N_TENSOR, QH_DEV * HD)
    wkv_single = w_keyvalue.reshape(D, N_TENSOR, HD)
    wkv_groups = jnp.concatenate([wkv_single, wkv_single], axis=2)

    def group_step(total, group):
        q_part = lax.dynamic_index_in_dim(query_groups, group, 1, keepdims=False)
        kv_part = lax.dynamic_index_in_dim(kv_groups, group, 1, keepdims=False)
        wq_part = lax.dynamic_index_in_dim(wq_groups, group, 1, keepdims=False)
        wkv_part = lax.dynamic_index_in_dim(wkv_groups, group, 1, keepdims=False)
        term = contract(q_part, wq_part, 1, 1) + contract(kv_part, wkv_part, 1, 1)
        return total + rounded(term), None

    hidden, unused_groups = lax.scan(group_step, jnp.zeros((TOKENS, D), jnp.float32), jnp.arange(N_TENSOR, dtype=jnp.int32))
    hidden_grad = hidden.astype(jnp.bfloat16)
    block = TOK_DEV * N_TENSOR

    def replica_step(totals, index):
        first_row = (index * block).astype(jnp.int32)
        x_rows = lax.dynamic_slice_in_dim(normed, first_row, block, 0)
        q_rows = lax.dynamic_slice_in_dim(query_grad, first_row, block, 0)
        kv_rows = lax.dynamic_slice_in_dim(keyvalue_grad, first_row, block, 0)
        a_rows = lax.dynamic_slice_in_dim(attn_out, first_row, block, 0)
        g_rows = lax.dynamic_slice_in_dim(out_grad, first_row, block, 0)
        q_part = contract(x_rows, q_rows, 0, 0)
        kv_full = contract(x_rows, kv_rows, 0, 0).reshape(D, KVH, 2, 2 * HD)
        kv_part = jnp.sum(kv_full, axis=2).reshape(D, 2 * KVH * HD)
        o_part = contract(a_rows, g_rows, 0, 0)
        return (totals[0] + rounded(q_part), totals[1] + rounded(kv_part), totals[2] + rounded(o_part)), None

    start_totals = (jnp.zeros((D, QH * HD), jnp.float32), jnp.zeros((D, 2 * KVH * HD), jnp.float32), jnp.zeros((QH * HD, D), jnp.float32))
    totals, unused = lax.scan(replica_step, start_totals, jnp.arange(N_DP, dtype=jnp.int32))
    return (hidden_grad, totals[0].astype(jnp.bfloat16), totals[1].astype(jnp.bfloat16), totals[2].astype(jnp.bfloat16))
```

```python
import functools

import jax
import jax.numpy as jnp
from jax import lax
from jax.experimental import pallas as pl
from jax.experimental.pallas import tpu as pltpu
from jax.sharding import PartitionSpec as P

MESH = pl.DeviceIdType.MESH
BF16 = jnp.bfloat16
F32 = jnp.float32

D = 4096
HD = 128
QW = 256
ROWS = QW + HD
TOK = 64
REP = 1024
BLK = 256
NZ = 8
NY = 4
AG_A = 2304
AG_B = D - AG_A
AG_B1 = 896
HR_A = 2304
HR_B = D - HR_A
HR_B1 = 896
SEMS = 112


def kernel(
    normed, out_grad, attn_out, d_query, d_keyvalue, cosine, sine, w_query, w_keyvalue,
    hidden_out, query_out, keyvalue_out, out_out,
    g_norm, g_out, w_cat, grads, h_grads, grads_t, attn_v, attn_t, q_in, kv_own, kv_other,
    cos_v, sin_v, part_h, rx_b, r2_a, r2_b1, r2_b2, ry_a, ry_b, rx_a, hs_a,
    ct_q, sb_q, rb_q, xs_q, xr_q, ct_o, sb_o, rb_o, xs_o, xr_o,
    send_sems, recv_sems, local_sems,
):
    dp = lax.axis_index("dp")
    tensor = lax.axis_index("tensor")
    c = tensor % 2
    y = (tensor // 2) % NY
    x = tensor // (2 * NY)
    z = dp % NZ
    h = dp // NZ
    xp = 1 - x
    yp, ym, y2 = (y + 1) % NY, (y + 3) % NY, (y + 2) % NY

    def tid(x_, y_, c_):
        return (x_ * NY + y_) * 2 + c_

    dev_x = (dp, tid(xp, y, c))
    dev_yp = (dp, tid(x, yp, c))
    dev_ym = (dp, tid(x, ym, c))
    dev_c = (dp, tid(x, y, 1 - c))
    dev_zp = (h * NZ + (z + 1) % NZ, tensor)
    dev_zm = (h * NZ + (z + NZ - 1) % NZ, tensor)
    dev_h = ((1 - h) * NZ + z, tensor)
    partners = (dev_x, dev_yp, dev_ym, dev_c, dev_zp, dev_zm, dev_h)

    messages = []
    locals_ = []

    def send(src, dst, device):
        at = len(messages)
        copy = pltpu.make_async_remote_copy(
            src_ref=src, dst_ref=dst, send_sem=send_sems.at[at], recv_sem=recv_sems.at[at],
            device_id=device, device_id_type=MESH,
        )
        copy.start()
        messages.append(copy)
        return copy

    def load(src, dst):
        copy = pltpu.make_async_copy(src, dst, local_sems.at[len(locals_)])
        copy.start()
        locals_.append(copy)
        return copy

    def gather(src, g):
        m = {}
        ca, cb = pl.ds(0, AG_A), pl.ds(AG_A, AG_B)
        cb1, cb2 = pl.ds(AG_A, AG_B1), pl.ds(AG_A + AG_B1, AG_B - AG_B1)
        full = pl.ds(0, D)

        def at(x_, y_, cols):
            return g.at[pl.ds(pl.multiple_of(tid(x_, y_, c) * TOK, TOK), TOK), cols]

        def go(name, x_, y_, cols, device):
            m[name] = send(at(x_, y_, cols), at(x_, y_, cols), device)

        def arrive(*names):
            for name in names:
                m[name].wait_recv()

        def s0():
            m["X0"] = send(src.at[:, ca], at(x, y, ca), dev_x)
            m["P0"] = send(src.at[:, cb], at(x, y, cb), dev_yp)
            m["M0"] = send(src.at[:, cb], at(x, y, cb), dev_ym)
            m["X1"] = send(src.at[:, cb], at(x, y, cb), dev_x)
            m["P1"] = send(src.at[:, ca], at(x, y, ca), dev_yp)
            m["M1"] = send(src.at[:, ca], at(x, y, ca), dev_ym)
            m["C0"] = send(src, at(x, y, full), dev_c)
            m["L"] = load(src, at(x, y, full))

        def s1():
            arrive("P0", "M0")
            go("P2", x, ym, cb1, dev_yp)
            go("M2", x, yp, cb2, dev_ym)
            go("X2", x, yp, cb, dev_x)
            go("X3", x, ym, cb, dev_x)

        def s2():
            arrive("X0")
            go("P3", xp, y, ca, dev_yp)
            go("M3", xp, y, ca, dev_ym)

        def s3():
            arrive("P1", "M1")
            go("P4", x, ym, ca, dev_yp)
            go("C1", x, ym, full, dev_c)
            go("C2", x, yp, full, dev_c)

        def s4():
            arrive("X1")
            go("C3", xp, y, full, dev_c)

        def s5():
            arrive("P2", "M2")
            go("X4", x, y2, cb, dev_x)

        def s6():
            arrive("P3", "M3")
            go("M4", xp, yp, ca, dev_ym)

        def s7():
            arrive("X2", "X3")
            go("C6", xp, yp, full, dev_c)
            go("C5", xp, ym, full, dev_c)

        def s8():
            arrive("P4")
            go("C4", x, y2, full, dev_c)
            arrive("M4", "X4")
            go("C7", xp, y2, full, dev_c)

        def s9():
            m["L"].wait()
            arrive(*("C%d" % i for i in range(8)))

        return s0, s1, s2, s3, s4, s5, s6, s7, s8, s9

    def reduce_dp(lhs, g, ct, sb, rb, xs, xr):
        m = {}

        def part(k, hh):
            cols = pl.ds(pl.multiple_of((hh * NZ + (z + k) % NZ) * BLK, BLK), BLK)
            return jnp.dot(lhs[...], g[:, cols], preferred_element_type=F32).astype(BF16)

        def slot(k):
            return 3 - k

        def s1():
            sb[0] = part(4, 0)
            m["P1"] = send(sb.at[0], rb.at[0, 0, 0], dev_zp)
            sb[1] = part(4, 1)
            m["M1"] = send(sb.at[1], rb.at[1, 0, 1], dev_zm)

            def body(i, carry):
                j = i // 2
                hh = i % 2
                ct[j, hh] = part(NZ + 3 - j, hh)
                return carry

            lax.fori_loop(0, 14, body, 0)

        def add(dst, value):
            return (dst.astype(F32) + value.astype(F32)).astype(BF16)

        def s2():
            m["P1"].wait_recv()
            rb[0, 0, 0] = add(rb[0, 0, 0], ct[slot(3), 0])
            rb[0, 0, 1] = ct[slot(3), 1]
            m["P2"] = send(rb.at[0, 0], rb.at[0, 1], dev_zp)
            m["M1"].wait_recv()
            rb[1, 0, 1] = add(rb[1, 0, 1], ct[slot(-3), 1])
            rb[1, 0, 0] = ct[slot(-3), 0]
            m["M2"] = send(rb.at[1, 0], rb.at[1, 1], dev_zm)

        def mid(s):
            k = 5 - s
            m["P%d" % (s - 1)].wait_recv()
            for hh in range(2):
                rb[0, s - 2, hh] = add(rb[0, s - 2, hh], ct[slot(k), hh])
            m["P%d" % s] = send(rb.at[0, s - 2], rb.at[0, s - 1], dev_zp)
            m["M%d" % (s - 1)].wait_recv()
            for hh in range(2):
                rb[1, s - 2, hh] = add(rb[1, s - 2, hh], ct[slot(-k), hh])
            m["M%d" % s] = send(rb.at[1, s - 2], rb.at[1, s - 1], dev_zm)

        def total(hh):
            return ct[slot(0), hh].astype(F32) + rb[0, 3, hh].astype(F32) + rb[1, 3, hh].astype(F32)

        def s5():
            m["P4"].wait_recv()
            m["M4"].wait_recv()
            xs[...] = total(1 - h).astype(BF16)
            m["H"] = send(xs, xr, dev_h)

        def s6():
            m["H"].wait_recv()
            return total(h) + xr[...].astype(F32)

        return s1, s2, functools.partial(mid, 3), functools.partial(mid, 4), s5, s6

    def reduce_hidden():
        m = {}
        ca, cb = pl.ds(0, HR_A), pl.ds(HR_A, HR_B)
        cb1, cb2 = pl.ds(HR_A, HR_B1), pl.ds(HR_A + HR_B1, HR_B - HR_B1)
        p = part_h

        def at(x_, y_):
            return x_ * NY + y_

        def add(d, cols, value):
            p[d, :, cols] = (p[d, :, cols].astype(F32) + value.astype(F32)).astype(BF16)

        def s0():
            m["HX0"] = send(p.at[pl.ds(xp * NY, NY), :, cb], rx_b, dev_x)
            m["HP0"] = send(p.at[at(x, y2), :, ca], r2_a.at[0], dev_yp)
            m["HM0"] = send(p.at[at(xp, y2), :, ca], r2_a.at[1], dev_ym)
            m["HP2b"] = send(p.at[at(xp, yp), :, ca], ry_a.at[0, 1], dev_yp)
            m["HM2a"] = send(p.at[at(x, ym), :, ca], ry_a.at[1, 0], dev_ym)

        def s1():
            m["HP0"].wait_recv()
            add(at(x, yp), ca, r2_a[0])
            m["HP2a"] = send(p.at[at(x, yp), :, ca], ry_a.at[0, 0], dev_yp)
            m["HM0"].wait_recv()
            add(at(xp, ym), ca, r2_a[1])
            m["HM2b"] = send(p.at[at(xp, ym), :, ca], ry_a.at[1, 1], dev_ym)

        def s2():
            m["HX0"].wait_recv()
            add(at(x, y2), cb, rx_b[y2])
            m["HP1"] = send(p.at[at(x, y2), :, cb1], r2_b1, dev_yp)
            m["HM1"] = send(p.at[at(x, y2), :, cb2], r2_b2, dev_ym)
            for y_ in (yp, ym, y):
                add(at(x, y_), cb, rx_b[y_])

        def s3():
            m["HP1"].wait_recv()
            add(at(x, yp), cb1, r2_b1[...])
            m["HP3"] = send(p.at[at(x, yp), :, cb], ry_b.at[0], dev_yp)
            m["HM1"].wait_recv()
            add(at(x, ym), cb2, r2_b2[...])
            m["HM3"] = send(p.at[at(x, ym), :, cb], ry_b.at[1], dev_ym)

        def s4():
            m["HP2b"].wait_recv()
            m["HM2b"].wait_recv()
            d = at(xp, y)
            hs_a[...] = (
                p[d, :, ca].astype(F32) + ry_a[0, 1].astype(F32) + ry_a[1, 1].astype(F32)
            ).astype(BF16)
            m["HX1"] = send(hs_a, rx_a, dev_x)

        def s5():
            for name in ("HP2a", "HM2a", "HP3", "HM3", "HX1"):
                m[name].wait_recv()
            d = at(x, y)
            hidden_out[:, ca] = (
                (p[d, :, ca].astype(F32) + ry_a[0, 0].astype(F32))
                + (ry_a[1, 0].astype(F32) + rx_a[...].astype(F32))
            ).astype(BF16)
            hidden_out[:, cb] = (
                p[d, :, cb].astype(F32) + ry_b[0].astype(F32) + ry_b[1].astype(F32)
            ).astype(BF16)

        return s0, s1, s2, s3, s4, s5

    def rotate_all():
        key = (1 - c).astype(F32)

        def body(d, carry):
            rows = pl.ds(pl.multiple_of(d * 2 * TOK, 2 * TOK), 2 * TOK)
            cs, sn = cos_v[rows, :], sin_v[rows, :]
            for head in range(QW // HD):
                cols = pl.ds(head * HD, HD)
                g = q_in[rows, cols].astype(F32)
                turned = g * cs + pltpu.roll(g, HD // 2, 1) * sn
                grads[d, :, :, cols] = turned.astype(BF16).reshape(2, TOK, HD)
            g = kv_own[rows, :].astype(F32) + kv_other[rows, :].astype(F32)
            cs, sn = cs * key + (1.0 - key), sn * key
            turned = g * cs + pltpu.roll(g, HD // 2, 1) * sn
            grads[d, :, :, pl.ds(QW, HD)] = turned.astype(BF16).reshape(2, TOK, HD)
            return carry

        lax.fori_loop(0, REP // (2 * TOK), body, 0)

    def transpose_all():
        def body(d, carry):
            cols = pl.ds(pl.multiple_of(d * 2 * TOK, 2 * TOK), 2 * TOK)
            grads_t[:, cols] = grads[d].reshape(2 * TOK, ROWS).T
            attn_t[:, cols] = attn_v[cols, :].T
            return carry

        lax.fori_loop(0, REP // (2 * TOK), body, 0)

    def hidden_partials():
        step = 512

        def body(i, carry):
            cols = pl.ds(pl.multiple_of(i * step, step), step)
            total = lax.dot_general(
                h_grads[...].reshape(REP // 2, 2 * ROWS), w_cat[cols, :],
                (((1,), (1,)), ((), ())), preferred_element_type=F32,
            )
            part_h[:, :, cols] = total.astype(BF16).reshape(2 * NY, TOK, step)
            return carry

        lax.fori_loop(0, D // step, body, 0)

    barrier = pltpu.get_barrier_semaphore()
    for device in partners:
        pl.semaphore_signal(barrier, inc=1, device_id=device, device_id_type=MESH)
    l_cos = load(cosine, cos_v)
    l_sin = load(sine, sin_v)
    l_q = load(d_query, q_in)
    l_kv = load(d_keyvalue.at[:, pl.ds(pl.multiple_of(c * HD, HD), HD)], kv_own)
    l_attn = load(attn_out, attn_v)
    l_wq = load(w_query, w_cat.at[:, pl.ds(0, QW)])
    l_wkv = load(w_keyvalue, w_cat.at[:, pl.ds(QW, HD)])
    pl.semaphore_wait(barrier, len(partners))

    a1 = gather(normed, g_norm)
    a2 = gather(out_grad, g_out)
    r1 = reduce_dp(grads_t, g_norm, ct_q, sb_q, rb_q, xs_q, xr_q)
    r2 = reduce_dp(attn_t, g_out, ct_o, sb_o, rb_o, xs_o, xr_o)
    hr = reduce_hidden()

    k_kv = send(
        d_keyvalue.at[:, pl.ds(pl.multiple_of((1 - c) * HD, HD), HD)], kv_other, dev_c
    )
    a1[0]()
    k_wq = send(w_query, w_cat.at[:, pl.ds(ROWS, QW)], dev_c)
    k_wkv = send(w_keyvalue, w_cat.at[:, pl.ds(ROWS + QW, HD)], dev_c)
    for copy in (l_cos, l_sin, l_q, l_kv):
        copy.wait()
    k_kv.wait_recv()
    rotate_all()
    k_g = send(grads.at[:, 1 - c], h_grads.at[:, :, pl.ds(ROWS, ROWS)], dev_c)
    l_g = load(grads.at[:, c], h_grads.at[:, :, pl.ds(0, ROWS)])
    a1[1]()
    a1[2]()
    l_attn.wait()
    transpose_all()
    a1[3]()
    a1[4]()
    a1[5]()
    a1[6]()
    a2[0]()
    for copy in (l_wq, l_wkv, l_g):
        copy.wait()
    for copy in (k_wq, k_wkv, k_g):
        copy.wait_recv()
    hidden_partials()
    a1[7]()
    a1[8]()
    a1[9]()
    r1[0]()
    a2[1]()
    a2[2]()
    r1[1]()
    a2[3]()
    a2[4]()
    a2[5]()
    r1[2]()
    a2[6]()
    hr[0]()
    a2[7]()
    a2[8]()
    a2[9]()
    r2[0]()
    r1[3]()
    hr[1]()
    r2[1]()
    hr[2]()
    r1[4]()
    r2[2]()
    hr[3]()
    total = r1[5]()
    query_out[...] = total[:QW].T.astype(BF16)
    keyvalue_out[...] = total[QW:].T.astype(BF16)
    hr[4]()
    r2[3]()
    r2[4]()
    hr[5]()
    out_out[...] = r2[5]().astype(BF16)
    for message in messages:
        message.wait_send()


def rotary_tables(positions):
    half = HD // 2
    inverse = jnp.power(F32(1000000.0), -(jnp.arange(half, dtype=F32) * 2.0 / HD))
    angles = positions.astype(F32)[:, None] * inverse[None, :]
    cosine, sine = jnp.cos(angles), jnp.sin(angles)
    return jnp.concatenate([cosine, cosine], axis=1), jnp.concatenate([sine, -sine], axis=1)


def local(normed, out_grad, attn_out, d_query, d_keyvalue, positions, w_query, w_keyvalue):
    cosine, sine = rotary_tables(positions)
    vmem = pltpu.VMEM
    return pl.pallas_call(
        kernel,
        out_shape=(
            jax.ShapeDtypeStruct((TOK, D), BF16),
            jax.ShapeDtypeStruct((BLK, QW), BF16),
            jax.ShapeDtypeStruct((BLK, HD), BF16),
            jax.ShapeDtypeStruct((QW, BLK), BF16),
        ),
        in_specs=[pl.BlockSpec(memory_space=pl.ANY)] * 9,
        out_specs=[pl.BlockSpec(memory_space=vmem)] * 4,
        scratch_shapes=[
            vmem((REP, D), BF16),
            vmem((REP, D), BF16),
            vmem((D, 2 * ROWS), BF16),
            vmem((2 * NY, 2, TOK, ROWS), BF16),
            vmem((2 * NY, TOK, 2 * ROWS), BF16),
            vmem((ROWS, REP), BF16),
            vmem((REP, QW), BF16),
            vmem((QW, REP), BF16),
            vmem((REP, QW), BF16),
            vmem((REP, HD), BF16),
            vmem((REP, HD), BF16),
            vmem((REP, HD), F32),
            vmem((REP, HD), F32),
            vmem((2 * NY, TOK, D), BF16),
            vmem((NY, TOK, HR_B), BF16),
            vmem((2, TOK, HR_A), BF16),
            vmem((TOK, HR_B1), BF16),
            vmem((TOK, HR_B - HR_B1), BF16),
            vmem((2, 2, TOK, HR_A), BF16),
            vmem((2, TOK, HR_B), BF16),
            vmem((TOK, HR_A), BF16),
            vmem((TOK, HR_A), BF16),
        ]
        + [
            shape
            for rows in (ROWS, QW)
            for shape in (
                vmem((7, 2, rows, BLK), BF16),
                vmem((2, rows, BLK), BF16),
                vmem((2, 4, 2, rows, BLK), BF16),
                vmem((rows, BLK), BF16),
                vmem((rows, BLK), BF16),
            )
        ]
        + [
            pltpu.SemaphoreType.DMA((SEMS,)),
            pltpu.SemaphoreType.DMA((SEMS,)),
            pltpu.SemaphoreType.DMA((16,)),
        ],
        compiler_params=pltpu.CompilerParams(
            collective_id=0, has_side_effects=True, vmem_limit_bytes=60 * 1024 * 1024
        ),
    )(normed, out_grad, attn_out, d_query, d_keyvalue, cosine, sine, w_query, w_keyvalue)


def solution(mesh):
    return jax.shard_map(
        local,
        mesh=mesh,
        in_specs=(
            P(("dp", "tensor"), None),
            P(("dp", "tensor"), None),
            P("dp", "tensor"),
            P("dp", "tensor"),
            P("dp", "tensor"),
            P("dp"),
            P(None, "tensor"),
            P(None, "tensor"),
        ),
        out_specs=(
            P(("dp", "tensor"), None),
            P("dp", "tensor"),
            P("dp", "tensor"),
            P("tensor", "dp"),
        ),
        check_vma=False,
    )
```

```python
import functools

import jax
import jax.numpy as jnp
from jax import lax
from jax.experimental import pallas as pl
from jax.experimental.pallas import tpu as pltpu
from jax.sharding import PartitionSpec as P

MESH = pl.DeviceIdType.MESH
BF16 = jnp.bfloat16
F32 = jnp.float32

D = 4096
HD = 128
QW = 256
ROWS = QW + HD
TOK = 64
REP = 1024
LOG_BASE = 13.815510557964274
BLK = 256
NZ = 8
NY = 4
ORDER = (4, 3, -3, 2, -2, 1, -1, 0)
SLOTS = 2 * NZ
PHASES = {1: ((0, 5, 3), (8, 4, 4)), 2: ((0, 4, 4), (8, 5, 3))}
HR_A = 2816
HR_B = D - HR_A
HR_B1 = 640
SEMS = 160
LOCAL_SEMS = 48

PLAN = (
    99, 0, 1, 100, 101, 2, 102, 3, 5, 4, 6, 12, 7, 8, 13, 103, 9, 104, 10, 105, 106, 14, 15, 17,
    11, 48, 16, 49, 18, 24, 57, 50, 58, 51, 19, 25, 20, 21, 56, 59, 22, 23, 26, 27, 61, 52, 62,
    53, 28, 29, 54, 30, 36, 60, 63, 55, 31, 37, 65, 33, 32, 66, 34, 38, 64, 67, 35, 69, 70, 39,
    78, 40, 71, 42, 41, 90, 79, 72, 43, 91, 68, 44, 45, 77, 46, 80, 47, 73, 82, 92, 83, 74, 75,
    76, 81, 84, 94, 93, 86, 87, 96, 85, 88, 89, 95, 97, 107, 108, 98,
)


def kernel(
    normed, out_grad, attn_out, d_query, d_keyvalue, positions, w_query, w_keyvalue,
    hidden_out, query_out, keyvalue_out, out_out,
    g_norm, g_out, w_cat, grads, h_grads, grads_t, attn_v, attn_t, q_in, kv_own, kv_other,
    pos_v, part_h, rx_b, r2_a, r2_b1, r2_b2, ry_a, ry_b, rx_a, hs_a,
    ct_q, sb_q, rb_q, xs_q, xr_q, ct_o, sb_o, rb_o, xs_o, xr_o,
    send_sems, recv_sems, local_sems,
):
    dp = lax.axis_index("dp")
    tensor = lax.axis_index("tensor")
    c = tensor % 2
    y = (tensor // 2) % NY
    x = tensor // (2 * NY)
    z = dp % NZ
    h = dp // NZ
    xp = 1 - x
    yp, ym, y2 = (y + 1) % NY, (y + 3) % NY, (y + 2) % NY

    def tid(x_, y_, c_):
        return (x_ * NY + y_) * 2 + c_

    dev_x = (dp, tid(xp, y, c))
    dev_yp = (dp, tid(x, yp, c))
    dev_ym = (dp, tid(x, ym, c))
    dev_c = (dp, tid(x, y, 1 - c))
    dev_zp = (h * NZ + (z + 1) % NZ, tensor)
    dev_zm = (h * NZ + (z + NZ - 1) % NZ, tensor)
    dev_h = ((1 - h) * NZ + z, tensor)
    partners = (dev_x, dev_yp, dev_ym, dev_c, dev_zp, dev_zm, dev_h)

    messages = []
    locals_ = []

    def send(src, dst, device):
        at = len(messages)
        copy = pltpu.make_async_remote_copy(
            src_ref=src, dst_ref=dst, send_sem=send_sems.at[at], recv_sem=recv_sems.at[at],
            device_id=device, device_id_type=MESH,
        )
        copy.start()
        messages.append(copy)
        return copy

    def load(src, dst):
        copy = pltpu.make_async_copy(src, dst, local_sems.at[len(locals_)])
        copy.start()
        locals_.append(copy)
        return copy

    def columns(j, hh):
        return pl.ds(pl.multiple_of((hh * NZ + (z + NZ + ORDER[j]) % NZ) * BLK, BLK), BLK)

    def load_own(src, g):
        rows = pl.ds(pl.multiple_of(tensor * TOK, TOK), TOK)
        return [
            load(src.at[:, columns(i // 2, i % 2)], g.at[i, rows, :]) for i in range(SLOTS)
        ]

    def gather(g, own, phase, steps):
        first, count_a, count_b = phase
        m = {}
        ca, cb = pl.ds(first, count_a), pl.ds(first + count_a, count_b)
        full = pl.ds(first, count_a + count_b)

        def go(name, x_, y_, slots, device, part=None):
            row = tid(x_, y_, c) * TOK
            size = TOK if part is None else TOK // 2
            row = pl.multiple_of(row + (size if part else 0), TOK // 2)
            ref = g.at[slots, pl.ds(row, size), :]
            m[name] = send(ref, ref, device)

        def arrive(*names):
            for name in names:
                m[name].wait_recv()

        def ownx():
            for copy in own[first:first + count_a + count_b]:
                copy.wait()
            go("X0", x, y, ca, dev_x)
            go("X1", x, y, cb, dev_x)

        def own_y():
            go("P0", x, y, cb, dev_yp)
            go("M0", x, y, cb, dev_ym)
            go("P1", x, y, ca, dev_yp)
            go("M1", x, y, ca, dev_ym)
            go("C0", x, y, full, dev_c)

        def p0():
            arrive("P0", "M0")
            go("P2", x, ym, cb, dev_yp, 0)
            go("M2", x, yp, cb, dev_ym, 1)
            go("X3", x, ym, cb, dev_x)
            go("X2", x, yp, cb, dev_x)

        def x0():
            arrive("X0")
            go("P3", xp, y, ca, dev_yp)
            go("M3", xp, y, ca, dev_ym)

        def p1():
            arrive("P1", "M1")
            go("P4", x, ym, ca, dev_yp, 0)
            go("M4", x, yp, ca, dev_ym, 1)
            go("C1", x, ym, full, dev_c)
            go("C2", x, yp, full, dev_c)

        def x1():
            arrive("X1")
            go("C3", xp, y, full, dev_c)

        def p2():
            arrive("P2", "M2")
            go("X4", x, y2, cb, dev_x, 0)
            go("X5", x, y2, cb, dev_x, 1)

        def p3():
            arrive("P3", "M3")
            go("P5", xp, ym, ca, dev_yp, 0)
            go("M5", xp, yp, ca, dev_ym, 1)

        def c6():
            arrive("X2", "X3")
            go("C6", xp, yp, full, dev_c)
            go("C5", xp, ym, full, dev_c)

        def c4():
            arrive("P4", "M4")
            go("C4", x, y2, full, dev_c)

        def c7():
            arrive("P5", "M5", "X4", "X5")
            go("C7", xp, y2, full, dev_c)

        def done():
            arrive(*("C%d" % i for i in range(8)))

        steps.extend((ownx, own_y, p0, x0, p1, x1, p2, p3, c6, c4, c7, done))

    def reduce_dp(lhs, g, ct, sb, rb, xs, xr, steps):
        m = {}

        def product(i):
            return jnp.dot(lhs[...], g[i], preferred_element_type=F32).astype(BF16)

        def first():
            sb[0] = product(0)
            m["P1", 0] = send(sb.at[0], rb.at[0, 0, 0], dev_zp)
            sb[1] = product(1)
            m["M1", 1] = send(sb.at[1], rb.at[1, 0, 1], dev_zm)

        def part(j):
            def body(hh, carry):
                ct[j - 1, hh] = product(2 * j + hh)
                return carry

            lax.fori_loop(0, 2, body, 0)

        def slot(k):
            return ORDER.index(k) - 1

        def forward(side, s, hh):
            k = 5 - s if side == "P" else s - 5
            d = 0 if side == "P" else 1
            if s == 2 and hh != d:
                source = ct.at[slot(k), hh]
            else:
                m[side + str(s - 1), hh].wait_recv()
                source = rb.at[d, s - 2, hh]
                source[...] = (source[...].astype(F32) + ct[slot(k), hh].astype(F32)).astype(BF16)
            m[side + str(s), hh] = send(
                source, rb.at[d, s - 1, hh], dev_zp if side == "P" else dev_zm
            )

        def total(hh):
            return ct[slot(0), hh].astype(F32) + rb[0, 3, hh].astype(F32) + rb[1, 3, hh].astype(F32)

        def exchange():
            for hh in range(2):
                m["P4", hh].wait_recv()
                m["M4", hh].wait_recv()
            xs[...] = total(1 - h).astype(BF16)
            m["H"] = send(xs, xr, dev_h)

        def finish():
            m["H"].wait_recv()
            return total(h) + xr[...].astype(F32)

        steps.append(first)
        steps.extend(functools.partial(part, j) for j in range(1, NZ))
        steps.extend(
            functools.partial(forward, side, s, hh)
            for s in (2, 3, 4) for side in "PM" for hh in range(2)
        )
        steps.append(exchange)
        return finish

    def reduce_hidden(steps):
        m = {}
        ca, cb = pl.ds(0, HR_A), pl.ds(HR_A, HR_B)
        cb1, cb2 = pl.ds(HR_A, HR_B1), pl.ds(HR_A + HR_B1, HR_B - HR_B1)
        p = part_h

        def at(x_, y_):
            return x_ * NY + y_

        def add(d, cols, value):
            p[d, :, cols] = (p[d, :, cols].astype(F32) + value.astype(F32)).astype(BF16)

        def hr0x():
            for i, y_ in enumerate((y2, yp, ym, y)):
                m["HX0", i] = send(p.at[at(xp, y_), :, cb], rx_b.at[i], dev_x)

        def hr0():
            m["HP0"] = send(p.at[at(x, y2), :, ca], r2_a.at[0], dev_yp)
            m["HM0"] = send(p.at[at(xp, y2), :, ca], r2_a.at[1], dev_ym)
            m["HP2b"] = send(p.at[at(xp, yp), :, ca], ry_a.at[0, 1], dev_yp)

        def hr1():
            m["HX0", 0].wait_recv()
            add(at(x, y2), cb, rx_b[0])
            m["HP1"] = send(p.at[at(x, y2), :, cb1], r2_b1, dev_yp)
            m["HM1"] = send(p.at[at(x, y2), :, cb2], r2_b2, dev_ym)

        def hr2m():
            m["HM0"].wait_recv()
            add(at(xp, ym), ca, r2_a[1])
            m["HM2b"] = send(p.at[at(xp, ym), :, ca], ry_a.at[1, 1], dev_ym)
            m["HM2a"] = send(p.at[at(x, ym), :, ca], ry_a.at[1, 0], dev_ym)

        def hr2p():
            m["HP0"].wait_recv()
            add(at(x, yp), ca, r2_a[0])
            m["HP2a"] = send(p.at[at(x, yp), :, ca], ry_a.at[0, 0], dev_yp)

        def hr3p():
            m["HX0", 1].wait_recv()
            add(at(x, yp), cb, rx_b[1])
            m["HP1"].wait_recv()
            add(at(x, yp), cb1, r2_b1[...])
            m["HP3"] = send(p.at[at(x, yp), :, cb], ry_b.at[0], dev_yp)

        def hr3m():
            m["HX0", 2].wait_recv()
            add(at(x, ym), cb, rx_b[2])
            m["HM1"].wait_recv()
            add(at(x, ym), cb2, r2_b2[...])
            m["HM3"] = send(p.at[at(x, ym), :, cb], ry_b.at[1], dev_ym)

        def hr4():
            m["HP2b"].wait_recv()
            m["HM2b"].wait_recv()
            d = at(xp, y)
            hs_a[...] = (
                p[d, :, ca].astype(F32) + ry_a[0, 1].astype(F32) + ry_a[1, 1].astype(F32)
            ).astype(BF16)
            m["HX1"] = send(hs_a, rx_a, dev_x)

        def hr5():
            d = at(x, y)
            m["HX0", 3].wait_recv()
            for name in ("HP2a", "HM2a", "HP3", "HM3", "HX1"):
                m[name].wait_recv()
            hidden_out[:, ca] = (
                (p[d, :, ca].astype(F32) + ry_a[0, 0].astype(F32))
                + (ry_a[1, 0].astype(F32) + rx_a[...].astype(F32))
            ).astype(BF16)
            hidden_out[:, cb] = (
                (p[d, :, cb].astype(F32) + rx_b[3].astype(F32))
                + (ry_b[0].astype(F32) + ry_b[1].astype(F32))
            ).astype(BF16)

        steps.extend((hr0x, hr0, hr1, hr2m, hr2p, hr3p, hr3m, hr4, hr5))

    def rotate_all():
        key = (1 - c).astype(F32)
        order = lax.broadcasted_iota(jnp.int32, (HD // 2, 2 * TOK), 0).astype(F32)
        inverse = jnp.exp(order * F32(-LOG_BASE * 2.0 / HD))

        def body(d, carry):
            rows = pl.ds(pl.multiple_of(d * 2 * TOK, 2 * TOK), 2 * TOK)
            angles = inverse * pos_v[pl.ds(d, 1), :].astype(F32)
            cs, sn = jnp.cos(angles), jnp.sin(angles)
            cs = jnp.concatenate([cs, cs], axis=0).T
            sn = jnp.concatenate([sn, -sn], axis=0).T
            for head in range(QW // HD):
                cols = pl.ds(head * HD, HD)
                g = q_in[rows, cols].astype(F32)
                turned = g * cs + pltpu.roll(g, HD // 2, 1) * sn
                grads[d, :, :, cols] = turned.astype(BF16).reshape(2, TOK, HD)
            g = kv_own[rows, :].astype(F32) + kv_other[rows, :].astype(F32)
            cs, sn = cs * key + (1.0 - key), sn * key
            turned = g * cs + pltpu.roll(g, HD // 2, 1) * sn
            grads[d, :, :, pl.ds(QW, HD)] = turned.astype(BF16).reshape(2, TOK, HD)
            return carry

        lax.fori_loop(0, REP // (2 * TOK), body, 0)

    def transpose_all():
        def body(d, carry):
            cols = pl.ds(pl.multiple_of(d * 2 * TOK, 2 * TOK), 2 * TOK)
            grads_t[:, cols] = grads[d].reshape(2 * TOK, ROWS).T
            attn_t[:, cols] = attn_v[cols, :].T
            return carry

        lax.fori_loop(0, REP // (2 * TOK), body, 0)

    def hidden_partials(first, last):
        step = 512

        def body(i, carry):
            cols = pl.ds(pl.multiple_of(i * step, step), step)
            total = lax.dot_general(
                h_grads[...].reshape(REP // 2, 2 * ROWS), w_cat[cols, :],
                (((1,), (1,)), ((), ())), preferred_element_type=F32,
            )
            part_h[:, :, cols] = total.astype(BF16).reshape(2 * NY, TOK, step)
            return carry

        lax.fori_loop(first, last, body, 0)

    barrier = pltpu.get_barrier_semaphore()
    for device in partners:
        pl.semaphore_signal(barrier, inc=1, device_id=device, device_id_type=MESH)
    own_norm = load_own(normed, g_norm)
    l_pos = load(positions, pos_v)
    l_q = load(d_query, q_in)
    l_kv = load(d_keyvalue.at[:, pl.ds(pl.multiple_of(c * HD, HD), HD)], kv_own)
    l_attn = load(attn_out, attn_v)
    l_wq = load(w_query, w_cat.at[:, pl.ds(0, QW)])
    l_wkv = load(w_keyvalue, w_cat.at[:, pl.ds(QW, HD)])
    own_out = load_own(out_grad, g_out)
    pl.semaphore_wait(barrier, len(partners))

    steps = []
    for n, g, own in ((1, g_norm, own_norm), (2, g_out, own_out)):
        for phase in PHASES[n]:
            gather(g, own, phase, steps)
    finish_1 = reduce_dp(grads_t, g_norm, ct_q, sb_q, rb_q, xs_q, xr_q, steps)
    finish_2 = reduce_dp(attn_t, g_out, ct_o, sb_o, rb_o, xs_o, xr_o, steps)
    reduce_hidden(steps)
    held = {}

    def start():
        held["kv"] = send(
            d_keyvalue.at[:, pl.ds(pl.multiple_of((1 - c) * HD, HD), HD)], kv_other, dev_c
        )

    def weights():
        held["wq"] = send(w_query, w_cat.at[:, pl.ds(ROWS, QW)], dev_c)
        held["wkv"] = send(w_keyvalue, w_cat.at[:, pl.ds(ROWS + QW, HD)], dev_c)

    def rotate():
        for copy in (l_pos, l_q, l_kv):
            copy.wait()
        held["kv"].wait_recv()
        rotate_all()
        held["g"] = send(grads.at[:, 1 - c], h_grads.at[:, :, pl.ds(ROWS, ROWS)], dev_c)
        held["lg"] = load(grads.at[:, c], h_grads.at[:, :, pl.ds(0, ROWS)])

    def transpose():
        l_attn.wait()
        transpose_all()

    def hidden(i):
        if i == 0:
            for copy in (l_wq, l_wkv, held["lg"]):
                copy.wait()
            for name in ("wq", "wkv", "g"):
                held[name].wait_recv()
        hidden_partials(2 * i, 2 * i + 2)

    def finish_q():
        total = finish_1()
        query_out[...] = total[:QW].T.astype(BF16)
        keyvalue_out[...] = total[QW:].T.astype(BF16)

    def finish_o():
        out_out[...] = finish_2().astype(BF16)

    steps.extend((start, weights, rotate, transpose))
    steps.extend(functools.partial(hidden, i) for i in range(4))
    steps.extend((finish_q, finish_o))
    assert sorted(PLAN) == list(range(len(steps)))
    for at in PLAN:
        steps[at]()
    for message in messages:
        message.wait_send()


def place(*refs):
    for i in range(4):
        refs[4 + i][...] = refs[i][...]


def local(normed, out_grad, attn_out, d_query, d_keyvalue, positions, w_query, w_keyvalue):
    vmem = pltpu.VMEM
    shapes = (
        jax.ShapeDtypeStruct((TOK, D), BF16),
        jax.ShapeDtypeStruct((BLK, QW), BF16),
        jax.ShapeDtypeStruct((BLK, HD), BF16),
        jax.ShapeDtypeStruct((QW, BLK), BF16),
    )
    results = pl.pallas_call(
        kernel,
        out_shape=tuple(vmem(shape.shape, shape.dtype) for shape in shapes),
        in_specs=[pl.BlockSpec(memory_space=pl.ANY)] * 8,
        out_specs=[pl.BlockSpec(memory_space=vmem)] * 4,
        scratch_shapes=[
            vmem((SLOTS, REP, BLK), BF16),
            vmem((SLOTS, REP, BLK), BF16),
            vmem((D, 2 * ROWS), BF16),
            vmem((2 * NY, 2, TOK, ROWS), BF16),
            vmem((2 * NY, TOK, 2 * ROWS), BF16),
            vmem((ROWS, REP), BF16),
            vmem((REP, QW), BF16),
            vmem((QW, REP), BF16),
            vmem((REP, QW), BF16),
            vmem((REP, HD), BF16),
            vmem((REP, HD), BF16),
            vmem((8, REP // 8), jnp.int32),
            vmem((2 * NY, TOK, D), BF16),
            vmem((NY, TOK, HR_B), BF16),
            vmem((2, TOK, HR_A), BF16),
            vmem((TOK, HR_B1), BF16),
            vmem((TOK, HR_B - HR_B1), BF16),
            vmem((2, 2, TOK, HR_A), BF16),
            vmem((2, TOK, HR_B), BF16),
            vmem((TOK, HR_A), BF16),
            vmem((TOK, HR_A), BF16),
        ]
        + [
            shape
            for rows in (ROWS, QW)
            for shape in (
                vmem((7, 2, rows, BLK), BF16),
                vmem((2, rows, BLK), BF16),
                vmem((2, 4, 2, rows, BLK), BF16),
                vmem((rows, BLK), BF16),
                vmem((rows, BLK), BF16),
            )
        ]
        + [
            pltpu.SemaphoreType.DMA((SEMS,)),
            pltpu.SemaphoreType.DMA((SEMS,)),
            pltpu.SemaphoreType.DMA((LOCAL_SEMS,)),
        ],
        compiler_params=pltpu.CompilerParams(
            collective_id=0, has_side_effects=True, vmem_limit_bytes=60 * 1024 * 1024
        ),
    )(
        normed, out_grad, attn_out, d_query, d_keyvalue, positions.reshape(8, REP // 8),
        w_query, w_keyvalue,
    )
    return pl.pallas_call(
        place,
        out_shape=shapes,
        in_specs=[pl.BlockSpec(memory_space=vmem)] * 4,
        out_specs=[pl.BlockSpec(memory_space=vmem)] * 4,
    )(*(pltpu.with_memory_space_constraint(result, vmem) for result in results))


def solution(mesh):
    return jax.shard_map(
        local,
        mesh=mesh,
        in_specs=(
            P(("dp", "tensor"), None),
            P(("dp", "tensor"), None),
            P("dp", "tensor"),
            P("dp", "tensor"),
            P("dp", "tensor"),
            P("dp"),
            P(None, "tensor"),
            P(None, "tensor"),
        ),
        out_specs=(
            P(("dp", "tensor"), None),
            P("dp", "tensor"),
            P("dp", "tensor"),
            P("tensor", "dp"),
        ),
        check_vma=False,
    )
```

```python
import functools

import jax
import jax.numpy as jnp
from jax import lax
from jax.experimental import pallas as pl
from jax.experimental.pallas import tpu as pltpu
from jax.sharding import PartitionSpec as P

MESH = pl.DeviceIdType.MESH
BF16 = jnp.bfloat16
F32 = jnp.float32

D = 4096
HD = 128
QW = 256
ROWS = QW + HD
TOK = 64
REP = 1024
LOG_BASE = 13.815510557964274
BLK = 256
NZ = 8
NY = 4
ORDER = (4, 3, -3, 2, -2, 1, -1, 0)
SLOTS = 2 * NZ
PHASES = {1: ((0, 4, 4), (8, 5, 3)), 2: ((0, 3, 3), (6, 6, 4))}
HR_A = 2560
HR_B = D - HR_A
HR_B1 = 768
SEMS = 160
LAG = 30
LOCAL_SEMS = 48

PLAN = (
    100, 0, 1, 101, 102, 2, 3, 103, 5, 4, 6, 12, 13, 7, 9, 8, 104, 14, 105, 106, 107, 15, 16, 10,
    18, 17, 24, 25, 11, 48, 19, 49, 20, 57, 21, 50, 58, 51, 26, 27, 36, 28, 56, 22, 29, 59, 30,
    37, 23, 52, 53, 31, 32, 33, 61, 62, 54, 55, 38, 60, 39, 63, 41, 40, 65, 66, 34, 42, 90, 35,
    69, 64, 67, 70, 43, 91, 44, 78, 71, 45, 79, 46, 77, 47, 80, 72, 73, 92, 74, 75, 76, 68, 94,
    93, 82, 83, 81, 84, 96, 86, 87, 95, 97, 85, 88, 108, 89, 99, 98, 109,
)


def kernel(
    normed, out_grad, attn_out, d_query, d_keyvalue, positions, w_query, w_keyvalue,
    hidden_out, query_out, keyvalue_out, out_out,
    g_norm, g_out, w_cat, grads, h_grads, grads_t, attn_v, attn_t, q_in, kv_own, kv_other,
    pos_v, part_h, rx_b, r2_a, r2_b1, r2_b2, ry_a, ry_b, rx_a, hs_a,
    ct_q, sb_q, rb_q, xs_q, xr_q, ct_o, sb_o, rb_o, xs_o, xr_o,
    send_sems, recv_sems, local_sems,
):
    dp = lax.axis_index("dp")
    tensor = lax.axis_index("tensor")
    c = tensor % 2
    y = (tensor // 2) % NY
    x = tensor // (2 * NY)
    z = dp % NZ
    h = dp // NZ
    xp = 1 - x
    yp, ym, y2 = (y + 1) % NY, (y + 3) % NY, (y + 2) % NY

    def tid(x_, y_, c_):
        return (x_ * NY + y_) * 2 + c_

    dev_x = (dp, tid(xp, y, c))
    dev_yp = (dp, tid(x, yp, c))
    dev_ym = (dp, tid(x, ym, c))
    dev_c = (dp, tid(x, y, 1 - c))
    dev_zp = (h * NZ + (z + 1) % NZ, tensor)
    dev_zm = (h * NZ + (z + NZ - 1) % NZ, tensor)
    dev_h = ((1 - h) * NZ + z, tensor)
    partners = (dev_x, dev_yp, dev_ym, dev_c, dev_zp, dev_zm, dev_h)

    messages = []
    locals_ = []

    def send(src, dst, device):
        at = len(messages)
        copy = pltpu.make_async_remote_copy(
            src_ref=src, dst_ref=dst, send_sem=send_sems.at[at], recv_sem=recv_sems.at[at],
            device_id=device, device_id_type=MESH,
        )
        copy.start()
        messages.append(copy)
        return copy

    def load(src, dst):
        copy = pltpu.make_async_copy(src, dst, local_sems.at[len(locals_)])
        copy.start()
        locals_.append(copy)
        return copy

    def columns(j, hh):
        return pl.ds(pl.multiple_of((hh * NZ + (z + NZ + ORDER[j]) % NZ) * BLK, BLK), BLK)

    def load_own(src, g, own, first, last):
        rows = pl.ds(pl.multiple_of(tensor * TOK, TOK), TOK)
        own.extend(
            load(src.at[:, columns(i // 2, i % 2)], g.at[i, rows, :])
            for i in range(first, last)
        )

    def gather(g, own, phase, steps):
        first, count_a, count_b = phase
        m = {}
        ca, cb = pl.ds(first, count_a), pl.ds(first + count_a, count_b)
        full = pl.ds(first, count_a + count_b)

        def go(name, x_, y_, slots, device, part=None):
            row = tid(x_, y_, c) * TOK
            size = TOK if part is None else TOK // 2
            row = pl.multiple_of(row + (size if part else 0), TOK // 2)
            ref = g.at[slots, pl.ds(row, size), :]
            m[name] = send(ref, ref, device)

        def arrive(*names):
            for name in names:
                m[name].wait_recv()

        def ownx():
            for copy in own[first:first + count_a + count_b]:
                copy.wait()
            go("X0", x, y, ca, dev_x)
            go("X1", x, y, cb, dev_x)

        def own_y():
            go("P0", x, y, cb, dev_yp)
            go("M0", x, y, cb, dev_ym)
            go("P1", x, y, ca, dev_yp)
            go("M1", x, y, ca, dev_ym)
            go("C0", x, y, full, dev_c)

        def p0():
            arrive("P0", "M0")
            go("P2", x, ym, cb, dev_yp, 0)
            go("M2", x, yp, cb, dev_ym, 1)
            go("X3", x, ym, cb, dev_x)
            go("X2", x, yp, cb, dev_x)

        def x0():
            arrive("X0")
            go("P3", xp, y, ca, dev_yp)
            go("M3", xp, y, ca, dev_ym)

        def p1():
            arrive("P1", "M1")
            go("P4", x, ym, ca, dev_yp, 0)
            go("M4", x, yp, ca, dev_ym, 1)
            go("C1", x, ym, full, dev_c)
            go("C2", x, yp, full, dev_c)

        def x1():
            arrive("X1")
            go("C3", xp, y, full, dev_c)

        def p2():
            arrive("P2", "M2")
            go("X4", x, y2, cb, dev_x, 0)
            go("X5", x, y2, cb, dev_x, 1)

        def p3():
            arrive("P3", "M3")
            go("P5", xp, ym, ca, dev_yp, 0)
            go("M5", xp, yp, ca, dev_ym, 1)

        def c6():
            arrive("X2", "X3")
            go("C6", xp, yp, full, dev_c)
            go("C5", xp, ym, full, dev_c)

        def c4():
            arrive("P4", "M4")
            go("C4", x, y2, full, dev_c)

        def c7():
            arrive("P5", "M5", "X4", "X5")
            go("C7", xp, y2, full, dev_c)

        def done():
            arrive(*("C%d" % i for i in range(8)))

        steps.extend((ownx, own_y, p0, x0, p1, x1, p2, p3, c6, c4, c7, done))

    def reduce_dp(lhs, g, ct, sb, rb, xs, xr, steps):
        m = {}

        def product(i):
            return jnp.dot(lhs[...], g[i], preferred_element_type=F32).astype(BF16)

        def first():
            sb[0] = product(0)
            m["P1", 0] = send(sb.at[0], rb.at[0, 0, 0], dev_zp)
            sb[1] = product(1)
            m["M1", 1] = send(sb.at[1], rb.at[1, 0, 1], dev_zm)

        def part(j):
            def body(hh, carry):
                ct[j - 1, hh] = product(2 * j + hh)
                return carry

            lax.fori_loop(0, 2, body, 0)

        def slot(k):
            return ORDER.index(k) - 1

        def forward(side, s, hh):
            k = 5 - s if side == "P" else s - 5
            d = 0 if side == "P" else 1
            if s == 2 and hh != d:
                source = ct.at[slot(k), hh]
            else:
                m[side + str(s - 1), hh].wait_recv()
                source = rb.at[d, s - 2, hh]
                source[...] = (source[...].astype(F32) + ct[slot(k), hh].astype(F32)).astype(BF16)
            m[side + str(s), hh] = send(
                source, rb.at[d, s - 1, hh], dev_zp if side == "P" else dev_zm
            )

        def total(hh):
            return ct[slot(0), hh].astype(F32) + rb[0, 3, hh].astype(F32) + rb[1, 3, hh].astype(F32)

        def exchange():
            for hh in range(2):
                m["P4", hh].wait_recv()
                m["M4", hh].wait_recv()
            xs[...] = total(1 - h).astype(BF16)
            m["H"] = send(xs, xr, dev_h)

        def finish():
            m["H"].wait_recv()
            return total(h) + xr[...].astype(F32)

        steps.append(first)
        steps.extend(functools.partial(part, j) for j in range(1, NZ))
        steps.extend(
            functools.partial(forward, side, s, hh)
            for s in (2, 3, 4) for side in "PM" for hh in range(2)
        )
        steps.append(exchange)
        return finish

    def reduce_hidden(steps):
        m = {}
        ca, cb = pl.ds(0, HR_A), pl.ds(HR_A, HR_B)
        cb1, cb2 = pl.ds(HR_A, HR_B1), pl.ds(HR_A + HR_B1, HR_B - HR_B1)
        p = part_h

        def at(x_, y_):
            return x_ * NY + y_

        def add(d, cols, value):
            p[d, :, cols] = (p[d, :, cols].astype(F32) + value.astype(F32)).astype(BF16)

        def hr0x():
            for i, y_ in enumerate((y2, yp, ym, y)):
                m["HX0", i] = send(p.at[at(xp, y_), :, cb], rx_b.at[i], dev_x)

        def hr0():
            m["HP0"] = send(p.at[at(x, y2), :, ca], r2_a.at[0], dev_yp)
            m["HM0"] = send(p.at[at(xp, y2), :, ca], r2_a.at[1], dev_ym)
            m["HP2b"] = send(p.at[at(xp, yp), :, ca], ry_a.at[0, 1], dev_yp)

        def hr1():
            m["HX0", 0].wait_recv()
            add(at(x, y2), cb, rx_b[0])
            m["HP1"] = send(p.at[at(x, y2), :, cb1], r2_b1, dev_yp)
            m["HM1"] = send(p.at[at(x, y2), :, cb2], r2_b2, dev_ym)

        def hr2m():
            m["HM0"].wait_recv()
            add(at(xp, ym), ca, r2_a[1])
            m["HM2b"] = send(p.at[at(xp, ym), :, ca], ry_a.at[1, 1], dev_ym)
            m["HM2a"] = send(p.at[at(x, ym), :, ca], ry_a.at[1, 0], dev_ym)

        def hr2p():
            m["HP0"].wait_recv()
            add(at(x, yp), ca, r2_a[0])
            m["HP2a"] = send(p.at[at(x, yp), :, ca], ry_a.at[0, 0], dev_yp)

        def hr3p():
            m["HX0", 1].wait_recv()
            add(at(x, yp), cb, rx_b[1])
            m["HP1"].wait_recv()
            add(at(x, yp), cb1, r2_b1[...])
            m["HP3"] = send(p.at[at(x, yp), :, cb], ry_b.at[0], dev_yp)

        def hr3m():
            m["HX0", 2].wait_recv()
            add(at(x, ym), cb, rx_b[2])
            m["HM1"].wait_recv()
            add(at(x, ym), cb2, r2_b2[...])
            m["HM3"] = send(p.at[at(x, ym), :, cb], ry_b.at[1], dev_ym)

        def hr4():
            m["HP2b"].wait_recv()
            m["HM2b"].wait_recv()
            d = at(xp, y)
            hs_a[...] = (
                p[d, :, ca].astype(F32) + ry_a[0, 1].astype(F32) + ry_a[1, 1].astype(F32)
            ).astype(BF16)
            m["HX1"] = send(hs_a, rx_a, dev_x)

        def hr5b():
            d = at(x, y)
            m["HX0", 3].wait_recv()
            m["HP3"].wait_recv()
            m["HM3"].wait_recv()
            hidden_out[:, cb] = (
                (p[d, :, cb].astype(F32) + rx_b[3].astype(F32))
                + (ry_b[0].astype(F32) + ry_b[1].astype(F32))
            ).astype(BF16)

        def hr5a():
            d = at(x, y)
            for name in ("HP2a", "HM2a", "HX1"):
                m[name].wait_recv()
            hidden_out[:, ca] = (
                (p[d, :, ca].astype(F32) + ry_a[0, 0].astype(F32))
                + (ry_a[1, 0].astype(F32) + rx_a[...].astype(F32))
            ).astype(BF16)

        steps.extend((hr0x, hr0, hr1, hr2m, hr2p, hr3p, hr3m, hr4, hr5b, hr5a))

    def rotate_all():
        key = (1 - c).astype(F32)
        order = lax.broadcasted_iota(jnp.int32, (HD // 2, 2 * TOK), 0).astype(F32)
        inverse = jnp.exp(order * F32(-LOG_BASE * 2.0 / HD))

        def body(d, carry):
            rows = pl.ds(pl.multiple_of(d * 2 * TOK, 2 * TOK), 2 * TOK)
            angles = inverse * pos_v[pl.ds(d, 1), :].astype(F32)
            cs, sn = jnp.cos(angles), jnp.sin(angles)
            cs = jnp.concatenate([cs, cs], axis=0).T
            sn = jnp.concatenate([sn, -sn], axis=0).T
            for head in range(QW // HD):
                cols = pl.ds(head * HD, HD)
                g = q_in[rows, cols].astype(F32)
                turned = g * cs + pltpu.roll(g, HD // 2, 1) * sn
                grads[d, :, :, cols] = turned.astype(BF16).reshape(2, TOK, HD)
            g = kv_own[rows, :].astype(F32) + kv_other[rows, :].astype(F32)
            cs, sn = cs * key + (1.0 - key), sn * key
            turned = g * cs + pltpu.roll(g, HD // 2, 1) * sn
            grads[d, :, :, pl.ds(QW, HD)] = turned.astype(BF16).reshape(2, TOK, HD)
            return carry

        lax.fori_loop(0, REP // (2 * TOK), body, 0)

    def transpose_all():
        def body(d, carry):
            cols = pl.ds(pl.multiple_of(d * 2 * TOK, 2 * TOK), 2 * TOK)
            grads_t[:, cols] = grads[d].reshape(2 * TOK, ROWS).T
            attn_t[:, cols] = attn_v[cols, :].T
            return carry

        lax.fori_loop(0, REP // (2 * TOK), body, 0)

    def hidden_partials(first, last):
        step = 512

        def body(i, carry):
            cols = pl.ds(pl.multiple_of(i * step, step), step)
            total = lax.dot_general(
                h_grads[...].reshape(REP // 2, 2 * ROWS), w_cat[cols, :],
                (((1,), (1,)), ((), ())), preferred_element_type=F32,
            )
            part_h[:, :, cols] = total.astype(BF16).reshape(2 * NY, TOK, step)
            return carry

        lax.fori_loop(first, last, body, 0)

    barrier = pltpu.get_barrier_semaphore()
    for device in partners:
        pl.semaphore_signal(barrier, inc=1, device_id=device, device_id_type=MESH)
    own_norm, own_out, held = [], [], {}
    load_own(normed, g_norm, own_norm, 0, SLOTS // 2)

    steps = []
    for n, g, own in ((1, g_norm, own_norm), (2, g_out, own_out)):
        for phase in PHASES[n]:
            gather(g, own, phase, steps)
    finish_1 = reduce_dp(grads_t, g_norm, ct_q, sb_q, rb_q, xs_q, xr_q, steps)
    finish_2 = reduce_dp(attn_t, g_out, ct_o, sb_o, rb_o, xs_o, xr_o, steps)
    reduce_hidden(steps)
    def start():
        pl.semaphore_wait(barrier, len(partners))

    def weights():
        held["lkv"] = load(d_keyvalue.at[:, pl.ds(pl.multiple_of(c * HD, HD), HD)], kv_own)
        held["kv"] = send(
            d_keyvalue.at[:, pl.ds(pl.multiple_of((1 - c) * HD, HD), HD)], kv_other, dev_c
        )
        held["lpos"] = load(positions, pos_v)
        held["lq"] = load(d_query, q_in)
        load_own(normed, g_norm, own_norm, SLOTS // 2, SLOTS)
        held["lattn"] = load(attn_out, attn_v)
        held["lwq"] = load(w_query, w_cat.at[:, pl.ds(0, QW)])
        held["lwkv"] = load(w_keyvalue, w_cat.at[:, pl.ds(QW, HD)])
        held["wq"] = send(w_query, w_cat.at[:, pl.ds(ROWS, QW)], dev_c)
        held["wkv"] = send(w_keyvalue, w_cat.at[:, pl.ds(ROWS + QW, HD)], dev_c)
        load_own(out_grad, g_out, own_out, 0, SLOTS)

    def rotate():
        for name in ("lpos", "lq", "lkv"):
            held[name].wait()
        held["kv"].wait_recv()
        rotate_all()
        held["g"] = send(grads.at[:, 1 - c], h_grads.at[:, :, pl.ds(ROWS, ROWS)], dev_c)
        held["lg"] = load(grads.at[:, c], h_grads.at[:, :, pl.ds(0, ROWS)])

    def transpose():
        held["lattn"].wait()
        transpose_all()

    def hidden(i):
        if i == 0:
            for name in ("lwq", "lwkv", "lg"):
                held[name].wait()
            for name in ("wq", "wkv", "g"):
                held[name].wait_recv()
        hidden_partials(2 * i, 2 * i + 2)

    def finish_q():
        total = finish_1()
        query_out[...] = total[:QW].T.astype(BF16)
        keyvalue_out[...] = total[QW:].T.astype(BF16)

    def finish_o():
        out_out[...] = finish_2().astype(BF16)

    steps.extend((start, weights, rotate, transpose))
    steps.extend(functools.partial(hidden, i) for i in range(4))
    steps.extend((finish_q, finish_o))
    assert sorted(PLAN) == list(range(len(steps)))
    issued = []
    waited = 0
    for at in PLAN:
        steps[at]()
        issued.append(len(messages))
        if len(issued) > LAG:
            for message in messages[waited:issued[-1 - LAG]]:
                message.wait_send()
            waited = issued[-1 - LAG]
    for message in messages[waited:]:
        message.wait_send()


def place(*refs):
    for i in range(4):
        refs[4 + i][...] = refs[i][...]


def local(normed, out_grad, attn_out, d_query, d_keyvalue, positions, w_query, w_keyvalue):
    vmem = pltpu.VMEM
    shapes = (
        jax.ShapeDtypeStruct((TOK, D), BF16),
        jax.ShapeDtypeStruct((BLK, QW), BF16),
        jax.ShapeDtypeStruct((BLK, HD), BF16),
        jax.ShapeDtypeStruct((QW, BLK), BF16),
    )
    results = pl.pallas_call(
        kernel,
        out_shape=tuple(vmem(shape.shape, shape.dtype) for shape in shapes),
        in_specs=[pl.BlockSpec(memory_space=pl.ANY)] * 8,
        out_specs=[pl.BlockSpec(memory_space=vmem)] * 4,
        scratch_shapes=[
            vmem((SLOTS, REP, BLK), BF16),
            vmem((SLOTS, REP, BLK), BF16),
            vmem((D, 2 * ROWS), BF16),
            vmem((2 * NY, 2, TOK, ROWS), BF16),
            vmem((2 * NY, TOK, 2 * ROWS), BF16),
            vmem((ROWS, REP), BF16),
            vmem((REP, QW), BF16),
            vmem((QW, REP), BF16),
            vmem((REP, QW), BF16),
            vmem((REP, HD), BF16),
            vmem((REP, HD), BF16),
            vmem((8, REP // 8), jnp.int32),
            vmem((2 * NY, TOK, D), BF16),
            vmem((NY, TOK, HR_B), BF16),
            vmem((2, TOK, HR_A), BF16),
            vmem((TOK, HR_B1), BF16),
            vmem((TOK, HR_B - HR_B1), BF16),
            vmem((2, 2, TOK, HR_A), BF16),
            vmem((2, TOK, HR_B), BF16),
            vmem((TOK, HR_A), BF16),
            vmem((TOK, HR_A), BF16),
        ]
        + [
            shape
            for rows in (ROWS, QW)
            for shape in (
                vmem((7, 2, rows, BLK), BF16),
                vmem((2, rows, BLK), BF16),
                vmem((2, 4, 2, rows, BLK), BF16),
                vmem((rows, BLK), BF16),
                vmem((rows, BLK), BF16),
            )
        ]
        + [
            pltpu.SemaphoreType.DMA((SEMS,)),
            pltpu.SemaphoreType.DMA((SEMS,)),
            pltpu.SemaphoreType.DMA((LOCAL_SEMS,)),
        ],
        compiler_params=pltpu.CompilerParams(
            collective_id=0, has_side_effects=True, vmem_limit_bytes=60 * 1024 * 1024
        ),
    )(
        normed, out_grad, attn_out, d_query, d_keyvalue, positions.reshape(8, REP // 8),
        w_query, w_keyvalue,
    )
    return pl.pallas_call(
        place,
        out_shape=shapes,
        in_specs=[pl.BlockSpec(memory_space=vmem)] * 4,
        out_specs=[pl.BlockSpec(memory_space=vmem)] * 4,
    )(*(pltpu.with_memory_space_constraint(result, vmem) for result in results))


def solution(mesh):
    return jax.shard_map(
        local,
        mesh=mesh,
        in_specs=(
            P(("dp", "tensor"), None),
            P(("dp", "tensor"), None),
            P("dp", "tensor"),
            P("dp", "tensor"),
            P("dp", "tensor"),
            P("dp"),
            P(None, "tensor"),
            P(None, "tensor"),
        ),
        out_specs=(
            P(("dp", "tensor"), None),
            P("dp", "tensor"),
            P("dp", "tensor"),
            P("tensor", "dp"),
        ),
        check_vma=False,
    )
```

```python
import functools

import jax
import jax.numpy as jnp
from jax import lax
from jax.experimental import pallas as pl
from jax.experimental.pallas import tpu as pltpu
from jax.sharding import PartitionSpec as P

MESH = pl.DeviceIdType.MESH
BF16 = jnp.bfloat16
F32 = jnp.float32

D = 4096
HD = 128
QW = 256
ROWS = QW + HD
TOK = 64
REP = 1024
LOG_BASE = 13.815510557964274
BLK = 256
NZ = 8
NY = 4
ORDER = (4, 3, -3, 2, -2, 1, -1, 0)
SLOTS = 2 * NZ
PHASES = {1: ((0, 4, 4), (8, 5, 3)), 2: ((0, 2, 2), (4, 7, 5))}
HR_A = 2560
HR_B = D - HR_A
HR_B1 = 768
SEMS = 160
LAG = 30
LOCAL_SEMS = 48

PLAN = (
    100, 0, 1, 101, 102, 2, 3, 103, 5, 4, 6, 12, 13, 7, 9, 8, 104, 14, 105, 106, 107, 15, 24, 10,
    16, 25, 18, 17, 11, 48, 49, 57, 50, 19, 58, 51, 20, 21, 26, 27, 29, 36, 28, 37, 59, 56, 22,
    30, 31, 32, 33, 23, 61, 52, 62, 53, 54, 38, 55, 60, 39, 63, 41, 40, 65, 66, 34, 42, 90, 64,
    35, 67, 69, 70, 78, 43, 91, 44, 45, 46, 68, 47, 71, 79, 72, 80, 77, 92, 76, 74, 73, 82, 93,
    94, 75, 83, 81, 84, 96, 86, 87, 85, 97, 95, 88, 108, 89, 98, 99, 109,
)


def kernel(
    normed, out_grad, attn_out, d_query, d_keyvalue, positions, w_query, w_keyvalue,
    hidden_out, query_out, keyvalue_out, out_out,
    g_norm, g_out, w_cat, grads, h_grads, grads_t, attn_v, attn_t, q_in, kv_own, kv_other,
    pos_v, part_h, rx_b, r2_a, r2_b1, r2_b2, ry_a, ry_b, rx_a, hs_a,
    ct_q, sb_q, rb_q, xs_q, xr_q, ct_o, sb_o, rb_o, xs_o, xr_o,
    send_sems, recv_sems, local_sems, ready_z, ready_h,
):
    dp = lax.axis_index("dp")
    tensor = lax.axis_index("tensor")
    c = tensor % 2
    y = (tensor // 2) % NY
    x = tensor // (2 * NY)
    z = dp % NZ
    h = dp // NZ
    xp = 1 - x
    yp, ym, y2 = (y + 1) % NY, (y + 3) % NY, (y + 2) % NY

    def tid(x_, y_, c_):
        return (x_ * NY + y_) * 2 + c_

    dev_x = (dp, tid(xp, y, c))
    dev_yp = (dp, tid(x, yp, c))
    dev_ym = (dp, tid(x, ym, c))
    dev_c = (dp, tid(x, y, 1 - c))
    dev_zp = (h * NZ + (z + 1) % NZ, tensor)
    dev_zm = (h * NZ + (z + NZ - 1) % NZ, tensor)
    dev_h = ((1 - h) * NZ + z, tensor)

    def signal(sem, *devices):
        for device in devices:
            pl.semaphore_signal(sem, inc=1, device_id=device, device_id_type=MESH)

    messages = []
    locals_ = []

    def send(src, dst, device):
        at = len(messages)
        copy = pltpu.make_async_remote_copy(
            src_ref=src, dst_ref=dst, send_sem=send_sems.at[at], recv_sem=recv_sems.at[at],
            device_id=device, device_id_type=MESH,
        )
        copy.start()
        messages.append(copy)
        return copy

    def load(src, dst):
        copy = pltpu.make_async_copy(src, dst, local_sems.at[len(locals_)])
        copy.start()
        locals_.append(copy)
        return copy

    def columns(j, hh):
        return pl.ds(pl.multiple_of((hh * NZ + (z + NZ + ORDER[j]) % NZ) * BLK, BLK), BLK)

    def load_own(src, g, own, first, last):
        rows = pl.ds(pl.multiple_of(tensor * TOK, TOK), TOK)
        own.extend(
            load(src.at[:, columns(i // 2, i % 2)], g.at[i, rows, :])
            for i in range(first, last)
        )

    def gather(g, own, phase, steps):
        first, count_a, count_b = phase
        m = {}
        ca, cb = pl.ds(first, count_a), pl.ds(first + count_a, count_b)
        full = pl.ds(first, count_a + count_b)

        def go(name, x_, y_, slots, device, part=None):
            row = tid(x_, y_, c) * TOK
            size = TOK if part is None else TOK // 2
            row = pl.multiple_of(row + (size if part else 0), TOK // 2)
            ref = g.at[slots, pl.ds(row, size), :]
            m[name] = send(ref, ref, device)

        def arrive(*names):
            for name in names:
                m[name].wait_recv()

        def ownx():
            for copy in own[first:first + count_a + count_b]:
                copy.wait()
            go("X0", x, y, ca, dev_x)
            go("X1", x, y, cb, dev_x)

        def own_y():
            go("P0", x, y, cb, dev_yp)
            go("M0", x, y, cb, dev_ym)
            go("P1", x, y, ca, dev_yp)
            go("M1", x, y, ca, dev_ym)
            go("C0", x, y, full, dev_c)

        def p0():
            arrive("P0", "M0")
            go("P2", x, ym, cb, dev_yp, 0)
            go("M2", x, yp, cb, dev_ym, 1)
            go("X3", x, ym, cb, dev_x)
            go("X2", x, yp, cb, dev_x)

        def x0():
            arrive("X0")
            go("P3", xp, y, ca, dev_yp)
            go("M3", xp, y, ca, dev_ym)

        def p1():
            arrive("P1", "M1")
            go("P4", x, ym, ca, dev_yp, 0)
            go("M4", x, yp, ca, dev_ym, 1)
            go("C1", x, ym, full, dev_c)
            go("C2", x, yp, full, dev_c)

        def x1():
            arrive("X1")
            go("C3", xp, y, full, dev_c)

        def p2():
            arrive("P2", "M2")
            go("X4", x, y2, cb, dev_x, 0)
            go("X5", x, y2, cb, dev_x, 1)

        def p3():
            arrive("P3", "M3")
            go("P5", xp, ym, ca, dev_yp, 0)
            go("M5", xp, yp, ca, dev_ym, 1)

        def c6():
            arrive("X2", "X3")
            go("C6", xp, yp, full, dev_c)
            go("C5", xp, ym, full, dev_c)

        def c4():
            arrive("P4", "M4")
            go("C4", x, y2, full, dev_c)

        def c7():
            arrive("P5", "M5", "X4", "X5")
            go("C7", xp, y2, full, dev_c)

        def done():
            arrive(*("C%d" % i for i in range(8)))

        steps.extend((ownx, own_y, p0, x0, p1, x1, p2, p3, c6, c4, c7, done))

    def reduce_dp(lhs, g, ct, sb, rb, xs, xr, steps, reach):
        m = {}

        def product(i):
            return jnp.dot(lhs[...], g[i], preferred_element_type=F32).astype(BF16)

        def first():
            sb[0] = product(0)
            reach()
            m["P1", 0] = send(sb.at[0], rb.at[0, 0, 0], dev_zp)
            sb[1] = product(1)
            m["M1", 1] = send(sb.at[1], rb.at[1, 0, 1], dev_zm)

        def part(j):
            def body(hh, carry):
                ct[j - 1, hh] = product(2 * j + hh)
                return carry

            lax.fori_loop(0, 2, body, 0)

        def slot(k):
            return ORDER.index(k) - 1

        def forward(side, s, hh):
            k = 5 - s if side == "P" else s - 5
            d = 0 if side == "P" else 1
            if s == 2 and hh != d:
                source = ct.at[slot(k), hh]
            else:
                m[side + str(s - 1), hh].wait_recv()
                source = rb.at[d, s - 2, hh]
                source[...] = (source[...].astype(F32) + ct[slot(k), hh].astype(F32)).astype(BF16)
            m[side + str(s), hh] = send(
                source, rb.at[d, s - 1, hh], dev_zp if side == "P" else dev_zm
            )

        def total(hh):
            return ct[slot(0), hh].astype(F32) + rb[0, 3, hh].astype(F32) + rb[1, 3, hh].astype(F32)

        def exchange():
            for hh in range(2):
                m["P4", hh].wait_recv()
                m["M4", hh].wait_recv()
            xs[...] = total(1 - h).astype(BF16)
            m["H"] = send(xs, xr, dev_h)

        def finish():
            m["H"].wait_recv()
            return total(h) + xr[...].astype(F32)

        steps.append(first)
        steps.extend(functools.partial(part, j) for j in range(1, NZ))
        steps.extend(
            functools.partial(forward, side, s, hh)
            for s in (2, 3, 4) for side in "PM" for hh in range(2)
        )
        steps.append(exchange)
        return finish

    def reduce_hidden(steps):
        m = {}
        ca, cb = pl.ds(0, HR_A), pl.ds(HR_A, HR_B)
        cb1, cb2 = pl.ds(HR_A, HR_B1), pl.ds(HR_A + HR_B1, HR_B - HR_B1)
        p = part_h

        def at(x_, y_):
            return x_ * NY + y_

        def add(d, cols, value):
            p[d, :, cols] = (p[d, :, cols].astype(F32) + value.astype(F32)).astype(BF16)

        def hr0x():
            for i, y_ in enumerate((y2, yp, ym, y)):
                m["HX0", i] = send(p.at[at(xp, y_), :, cb], rx_b.at[i], dev_x)

        def hr0():
            m["HP0"] = send(p.at[at(x, y2), :, ca], r2_a.at[0], dev_yp)
            m["HM0"] = send(p.at[at(xp, y2), :, ca], r2_a.at[1], dev_ym)
            m["HP2b"] = send(p.at[at(xp, yp), :, ca], ry_a.at[0, 1], dev_yp)

        def hr1():
            m["HX0", 0].wait_recv()
            add(at(x, y2), cb, rx_b[0])
            m["HP1"] = send(p.at[at(x, y2), :, cb1], r2_b1, dev_yp)
            m["HM1"] = send(p.at[at(x, y2), :, cb2], r2_b2, dev_ym)

        def hr2m():
            m["HM0"].wait_recv()
            add(at(xp, ym), ca, r2_a[1])
            m["HM2b"] = send(p.at[at(xp, ym), :, ca], ry_a.at[1, 1], dev_ym)
            m["HM2a"] = send(p.at[at(x, ym), :, ca], ry_a.at[1, 0], dev_ym)

        def hr2p():
            m["HP0"].wait_recv()
            add(at(x, yp), ca, r2_a[0])
            m["HP2a"] = send(p.at[at(x, yp), :, ca], ry_a.at[0, 0], dev_yp)

        def hr3p():
            m["HX0", 1].wait_recv()
            add(at(x, yp), cb, rx_b[1])
            m["HP1"].wait_recv()
            add(at(x, yp), cb1, r2_b1[...])
            m["HP3"] = send(p.at[at(x, yp), :, cb], ry_b.at[0], dev_yp)

        def hr3m():
            m["HX0", 2].wait_recv()
            add(at(x, ym), cb, rx_b[2])
            m["HM1"].wait_recv()
            add(at(x, ym), cb2, r2_b2[...])
            m["HM3"] = send(p.at[at(x, ym), :, cb], ry_b.at[1], dev_ym)

        def hr4():
            m["HP2b"].wait_recv()
            m["HM2b"].wait_recv()
            d = at(xp, y)
            hs_a[...] = (
                p[d, :, ca].astype(F32) + ry_a[0, 1].astype(F32) + ry_a[1, 1].astype(F32)
            ).astype(BF16)
            m["HX1"] = send(hs_a, rx_a, dev_x)

        def hr5b():
            d = at(x, y)
            m["HX0", 3].wait_recv()
            m["HP3"].wait_recv()
            m["HM3"].wait_recv()
            hidden_out[:, cb] = (
                (p[d, :, cb].astype(F32) + rx_b[3].astype(F32))
                + (ry_b[0].astype(F32) + ry_b[1].astype(F32))
            ).astype(BF16)

        def hr5a():
            d = at(x, y)
            for name in ("HP2a", "HM2a", "HX1"):
                m[name].wait_recv()
            hidden_out[:, ca] = (
                (p[d, :, ca].astype(F32) + ry_a[0, 0].astype(F32))
                + (ry_a[1, 0].astype(F32) + rx_a[...].astype(F32))
            ).astype(BF16)

        steps.extend((hr0x, hr0, hr1, hr2m, hr2p, hr3p, hr3m, hr4, hr5b, hr5a))

    def rotate_all():
        key = (1 - c).astype(F32)
        order = lax.broadcasted_iota(jnp.int32, (HD // 2, 2 * TOK), 0).astype(F32)
        inverse = jnp.exp(order * F32(-LOG_BASE * 2.0 / HD))

        def body(d, carry):
            rows = pl.ds(pl.multiple_of(d * 2 * TOK, 2 * TOK), 2 * TOK)
            angles = inverse * pos_v[pl.ds(d, 1), :].astype(F32)
            cs, sn = jnp.cos(angles), jnp.sin(angles)
            cs = jnp.concatenate([cs, cs], axis=0).T
            sn = jnp.concatenate([sn, -sn], axis=0).T
            for head in range(QW // HD):
                cols = pl.ds(head * HD, HD)
                g = q_in[rows, cols].astype(F32)
                turned = g * cs + pltpu.roll(g, HD // 2, 1) * sn
                grads[d, :, :, cols] = turned.astype(BF16).reshape(2, TOK, HD)
            g = kv_own[rows, :].astype(F32) + kv_other[rows, :].astype(F32)
            cs, sn = cs * key + (1.0 - key), sn * key
            turned = g * cs + pltpu.roll(g, HD // 2, 1) * sn
            grads[d, :, :, pl.ds(QW, HD)] = turned.astype(BF16).reshape(2, TOK, HD)
            return carry

        lax.fori_loop(0, REP // (2 * TOK), body, 0)

    def transpose_all():
        def body(d, carry):
            cols = pl.ds(pl.multiple_of(d * 2 * TOK, 2 * TOK), 2 * TOK)
            grads_t[:, cols] = grads[d].reshape(2 * TOK, ROWS).T
            attn_t[:, cols] = attn_v[cols, :].T
            return carry

        lax.fori_loop(0, REP // (2 * TOK), body, 0)

    def hidden_partials(first, last):
        step = 512

        def body(i, carry):
            cols = pl.ds(pl.multiple_of(i * step, step), step)
            total = lax.dot_general(
                h_grads[...].reshape(REP // 2, 2 * ROWS), w_cat[cols, :],
                (((1,), (1,)), ((), ())), preferred_element_type=F32,
            )
            part_h[:, :, cols] = total.astype(BF16).reshape(2 * NY, TOK, step)
            return carry

        lax.fori_loop(first, last, body, 0)

    barrier = pltpu.get_barrier_semaphore()
    signal(barrier, dev_x, dev_yp, dev_ym, dev_c)
    pl.when(z % 2 == 0)(lambda: signal(barrier, dev_zp, dev_zm))
    pl.when(h == 0)(lambda: signal(barrier, dev_h))
    own_norm, own_out, held = [], [], {}
    load_own(normed, g_norm, own_norm, 0, SLOTS // 2)

    def reach_dp():
        pl.when(z % 2 == 0)(lambda: pl.semaphore_wait(ready_z, 2))
        pl.when(h == 0)(lambda: pl.semaphore_wait(ready_h, 1))

    steps = []
    for n, g, own in ((1, g_norm, own_norm), (2, g_out, own_out)):
        for phase in PHASES[n]:
            gather(g, own, phase, steps)
    finish_1 = reduce_dp(grads_t, g_norm, ct_q, sb_q, rb_q, xs_q, xr_q, steps, reach_dp)
    finish_2 = reduce_dp(attn_t, g_out, ct_o, sb_o, rb_o, xs_o, xr_o, steps, lambda: None)
    reduce_hidden(steps)
    def start():
        pl.semaphore_wait(barrier, 4 + 2 * (z % 2) + h)
        pl.when(z % 2 == 1)(lambda: signal(ready_z, dev_zp, dev_zm))
        pl.when(h == 1)(lambda: signal(ready_h, dev_h))

    def weights():
        held["lkv"] = load(d_keyvalue.at[:, pl.ds(pl.multiple_of(c * HD, HD), HD)], kv_own)
        held["kv"] = send(
            d_keyvalue.at[:, pl.ds(pl.multiple_of((1 - c) * HD, HD), HD)], kv_other, dev_c
        )
        held["lpos"] = load(positions, pos_v)
        held["lq"] = load(d_query, q_in)
        load_own(normed, g_norm, own_norm, SLOTS // 2, SLOTS)
        held["lattn"] = load(attn_out, attn_v)
        held["lwq"] = load(w_query, w_cat.at[:, pl.ds(0, QW)])
        held["lwkv"] = load(w_keyvalue, w_cat.at[:, pl.ds(QW, HD)])
        held["wq"] = send(w_query, w_cat.at[:, pl.ds(ROWS, QW)], dev_c)
        held["wkv"] = send(w_keyvalue, w_cat.at[:, pl.ds(ROWS + QW, HD)], dev_c)
        load_own(out_grad, g_out, own_out, 0, SLOTS)

    def rotate():
        for name in ("lpos", "lq", "lkv"):
            held[name].wait()
        held["kv"].wait_recv()
        rotate_all()
        held["g"] = send(grads.at[:, 1 - c], h_grads.at[:, :, pl.ds(ROWS, ROWS)], dev_c)
        held["lg"] = load(grads.at[:, c], h_grads.at[:, :, pl.ds(0, ROWS)])

    def transpose():
        held["lattn"].wait()
        transpose_all()

    def hidden(i):
        if i == 0:
            for name in ("lwq", "lwkv", "lg"):
                held[name].wait()
            for name in ("wq", "wkv", "g"):
                held[name].wait_recv()
        hidden_partials(2 * i, 2 * i + 2)

    def finish_q():
        total = finish_1()
        query_out[...] = total[:QW].T.astype(BF16)
        keyvalue_out[...] = total[QW:].T.astype(BF16)

    def finish_o():
        out_out[...] = finish_2().astype(BF16)

    steps.extend((start, weights, rotate, transpose))
    steps.extend(functools.partial(hidden, i) for i in range(4))
    steps.extend((finish_q, finish_o))
    assert sorted(PLAN) == list(range(len(steps)))
    issued = []
    waited = 0
    for at in PLAN:
        steps[at]()
        issued.append(len(messages))
        if len(issued) > LAG:
            for message in messages[waited:issued[-1 - LAG]]:
                message.wait_send()
            waited = issued[-1 - LAG]
    for message in messages[waited:]:
        message.wait_send()


def place(*refs):
    for i in range(4):
        refs[4 + i][...] = refs[i][...]


def local(normed, out_grad, attn_out, d_query, d_keyvalue, positions, w_query, w_keyvalue):
    vmem = pltpu.VMEM
    shapes = (
        jax.ShapeDtypeStruct((TOK, D), BF16),
        jax.ShapeDtypeStruct((BLK, QW), BF16),
        jax.ShapeDtypeStruct((BLK, HD), BF16),
        jax.ShapeDtypeStruct((QW, BLK), BF16),
    )
    results = pl.pallas_call(
        kernel,
        out_shape=tuple(vmem(shape.shape, shape.dtype) for shape in shapes),
        in_specs=[pl.BlockSpec(memory_space=pl.ANY)] * 8,
        out_specs=[pl.BlockSpec(memory_space=vmem)] * 4,
        scratch_shapes=[
            vmem((SLOTS, REP, BLK), BF16),
            vmem((SLOTS, REP, BLK), BF16),
            vmem((D, 2 * ROWS), BF16),
            vmem((2 * NY, 2, TOK, ROWS), BF16),
            vmem((2 * NY, TOK, 2 * ROWS), BF16),
            vmem((ROWS, REP), BF16),
            vmem((REP, QW), BF16),
            vmem((QW, REP), BF16),
            vmem((REP, QW), BF16),
            vmem((REP, HD), BF16),
            vmem((REP, HD), BF16),
            vmem((8, REP // 8), jnp.int32),
            vmem((2 * NY, TOK, D), BF16),
            vmem((NY, TOK, HR_B), BF16),
            vmem((2, TOK, HR_A), BF16),
            vmem((TOK, HR_B1), BF16),
            vmem((TOK, HR_B - HR_B1), BF16),
            vmem((2, 2, TOK, HR_A), BF16),
            vmem((2, TOK, HR_B), BF16),
            vmem((TOK, HR_A), BF16),
            vmem((TOK, HR_A), BF16),
        ]
        + [
            shape
            for rows in (ROWS, QW)
            for shape in (
                vmem((7, 2, rows, BLK), BF16),
                vmem((2, rows, BLK), BF16),
                vmem((2, 4, 2, rows, BLK), BF16),
                vmem((rows, BLK), BF16),
                vmem((rows, BLK), BF16),
            )
        ]
        + [
            pltpu.SemaphoreType.DMA((SEMS,)),
            pltpu.SemaphoreType.DMA((SEMS,)),
            pltpu.SemaphoreType.DMA((LOCAL_SEMS,)),
            pltpu.SemaphoreType.REGULAR,
            pltpu.SemaphoreType.REGULAR,
        ],
        compiler_params=pltpu.CompilerParams(
            collective_id=0, has_side_effects=True, vmem_limit_bytes=60 * 1024 * 1024
        ),
    )(
        normed, out_grad, attn_out, d_query, d_keyvalue, positions.reshape(8, REP // 8),
        w_query, w_keyvalue,
    )
    return pl.pallas_call(
        place,
        out_shape=shapes,
        in_specs=[pl.BlockSpec(memory_space=vmem)] * 4,
        out_specs=[pl.BlockSpec(memory_space=vmem)] * 4,
    )(*(pltpu.with_memory_space_constraint(result, vmem) for result in results))


def solution(mesh):
    return jax.shard_map(
        local,
        mesh=mesh,
        in_specs=(
            P(("dp", "tensor"), None),
            P(("dp", "tensor"), None),
            P("dp", "tensor"),
            P("dp", "tensor"),
            P("dp", "tensor"),
            P("dp"),
            P(None, "tensor"),
            P(None, "tensor"),
        ),
        out_specs=(
            P(("dp", "tensor"), None),
            P("dp", "tensor"),
            P("dp", "tensor"),
            P("tensor", "dp"),
        ),
        check_vma=False,
    )
```

```python
import functools

import jax
import jax.numpy as jnp
from jax import lax
from jax.experimental import pallas as pl
from jax.experimental.pallas import tpu as pltpu
from jax.sharding import PartitionSpec as P

MESH = pl.DeviceIdType.MESH
BF16 = jnp.bfloat16
F32 = jnp.float32

D = 4096
HD = 128
QW = 256
ROWS = QW + HD
TOK = 64
REP = 1024
LOG_BASE = 13.815510557964274
BLK = 256
NZ = 8
NY = 4
ORDER = (4, 3, -3, 2, -2, 1, -1, 0)
SLOTS = 2 * NZ
PHASES = {1: ((0, 4, 4), (8, 5, 3)), 2: ((0, 2, 2), (4, 7, 5))}
HR_A = 2560
HR_B = D - HR_A
HR_B1 = 768
SEMS = 160
LAG = 48
LOCAL_SEMS = 48

PLAN = (
    100, 0, 1, 101, 102, 2, 3, 103, 5, 4, 6, 12, 13, 7, 9, 8, 104, 14, 105, 106, 107, 15, 24, 10,
    16, 25, 18, 17, 11, 48, 49, 57, 50, 19, 58, 51, 20, 21, 26, 27, 29, 36, 28, 37, 59, 56, 22,
    30, 31, 32, 33, 23, 61, 52, 62, 53, 54, 38, 55, 60, 39, 63, 41, 40, 65, 66, 34, 42, 90, 64,
    35, 67, 69, 70, 78, 43, 91, 44, 45, 46, 68, 47, 71, 79, 72, 80, 77, 92, 76, 74, 73, 82, 93,
    94, 75, 83, 81, 84, 96, 86, 87, 85, 97, 95, 88, 108, 89, 98, 99, 109,
)


def kernel(
    normed, out_grad, attn_out, d_query, d_keyvalue, positions, w_query, w_keyvalue,
    hidden_out, query_out, keyvalue_out, out_out,
    g_norm, g_out, w_cat, grads, h_grads, grads_t, attn_v, attn_t, q_in, kv_own, kv_other,
    pos_v, part_h, rx_b, r2_a, r2_b1, r2_b2, ry_a, ry_b, rx_a, hs_a,
    ct_q, sb_q, rb_q, xs_q, xr_q, ct_o, sb_o, rb_o, xs_o, xr_o,
    send_sems, recv_sems, local_sems, ready_z, ready_h,
):
    dp = lax.axis_index("dp")
    tensor = lax.axis_index("tensor")
    c = tensor % 2
    y = (tensor // 2) % NY
    x = tensor // (2 * NY)
    z = dp % NZ
    h = dp // NZ
    xp = 1 - x
    yp, ym, y2 = (y + 1) % NY, (y + 3) % NY, (y + 2) % NY

    def tid(x_, y_, c_):
        return (x_ * NY + y_) * 2 + c_

    dev_x = (dp, tid(xp, y, c))
    dev_yp = (dp, tid(x, yp, c))
    dev_ym = (dp, tid(x, ym, c))
    dev_c = (dp, tid(x, y, 1 - c))
    dev_zp = (h * NZ + (z + 1) % NZ, tensor)
    dev_zm = (h * NZ + (z + NZ - 1) % NZ, tensor)
    dev_h = ((1 - h) * NZ + z, tensor)

    def signal(sem, *devices):
        for device in devices:
            pl.semaphore_signal(sem, inc=1, device_id=device, device_id_type=MESH)

    messages = []
    locals_ = []

    def send(src, dst, device):
        at = len(messages)
        copy = pltpu.make_async_remote_copy(
            src_ref=src, dst_ref=dst, send_sem=send_sems.at[at], recv_sem=recv_sems.at[at],
            device_id=device, device_id_type=MESH,
        )
        copy.start()
        messages.append(copy)
        return copy

    def load(src, dst):
        copy = pltpu.make_async_copy(src, dst, local_sems.at[len(locals_)])
        copy.start()
        locals_.append(copy)
        return copy

    def columns(j, hh):
        return pl.ds(pl.multiple_of((hh * NZ + (z + NZ + ORDER[j]) % NZ) * BLK, BLK), BLK)

    def load_own(src, g, own, first, last):
        rows = pl.ds(pl.multiple_of(tensor * TOK, TOK), TOK)
        own.extend(
            load(src.at[:, columns(i // 2, i % 2)], g.at[i, rows, :])
            for i in range(first, last)
        )

    def gather(g, own, phase, steps):
        first, count_a, count_b = phase
        m = {}
        ca, cb = pl.ds(first, count_a), pl.ds(first + count_a, count_b)
        full = pl.ds(first, count_a + count_b)

        def go(name, x_, y_, slots, device, part=None):
            row = tid(x_, y_, c) * TOK
            size = TOK if part is None else TOK // 2
            row = pl.multiple_of(row + (size if part else 0), TOK // 2)
            ref = g.at[slots, pl.ds(row, size), :]
            m[name] = send(ref, ref, device)

        def arrive(*names):
            for name in names:
                m[name].wait_recv()

        def ownx():
            for copy in own[first:first + count_a + count_b]:
                copy.wait()
            go("X0", x, y, ca, dev_x)
            go("X1", x, y, cb, dev_x)

        def own_y():
            go("P0", x, y, cb, dev_yp)
            go("M0", x, y, cb, dev_ym)
            go("P1", x, y, ca, dev_yp)
            go("M1", x, y, ca, dev_ym)
            go("C0", x, y, full, dev_c)

        def p0():
            arrive("P0", "M0")
            go("P2", x, ym, cb, dev_yp, 0)
            go("M2", x, yp, cb, dev_ym, 1)
            go("X3", x, ym, cb, dev_x)
            go("X2", x, yp, cb, dev_x)

        def x0():
            arrive("X0")
            go("P3", xp, y, ca, dev_yp)
            go("M3", xp, y, ca, dev_ym)

        def p1():
            arrive("P1", "M1")
            go("P4", x, ym, ca, dev_yp, 0)
            go("M4", x, yp, ca, dev_ym, 1)
            go("C1", x, ym, full, dev_c)
            go("C2", x, yp, full, dev_c)

        def x1():
            arrive("X1")
            go("C3", xp, y, full, dev_c)

        def p2():
            arrive("P2", "M2")
            go("X4", x, y2, cb, dev_x, 0)
            go("X5", x, y2, cb, dev_x, 1)

        def p3():
            arrive("P3", "M3")
            go("P5", xp, ym, ca, dev_yp, 0)
            go("M5", xp, yp, ca, dev_ym, 1)

        def c6():
            arrive("X2", "X3")
            go("C6", xp, yp, full, dev_c)
            go("C5", xp, ym, full, dev_c)

        def c4():
            arrive("P4", "M4")
            go("C4", x, y2, full, dev_c)

        def c7():
            arrive("P5", "M5", "X4", "X5")
            go("C7", xp, y2, full, dev_c)

        def done():
            arrive(*("C%d" % i for i in range(8)))

        steps.extend((ownx, own_y, p0, x0, p1, x1, p2, p3, c6, c4, c7, done))

    def reduce_dp(lhs, g, ct, sb, rb, xs, xr, steps, reach):
        m = {}

        def product(i):
            return jnp.dot(lhs[...], g[i], preferred_element_type=F32).astype(BF16)

        def first():
            sb[0] = product(0)
            reach()
            m["P1", 0] = send(sb.at[0], rb.at[0, 0, 0], dev_zp)
            sb[1] = product(1)
            m["M1", 1] = send(sb.at[1], rb.at[1, 0, 1], dev_zm)

        def part(j):
            def body(hh, carry):
                ct[j - 1, hh] = product(2 * j + hh)
                return carry

            lax.fori_loop(0, 2, body, 0)

        def slot(k):
            return ORDER.index(k) - 1

        def forward(side, s, hh):
            k = 5 - s if side == "P" else s - 5
            d = 0 if side == "P" else 1
            if s == 2 and hh != d:
                source = ct.at[slot(k), hh]
            else:
                m[side + str(s - 1), hh].wait_recv()
                source = rb.at[d, s - 2, hh]
                source[...] = (source[...].astype(F32) + ct[slot(k), hh].astype(F32)).astype(BF16)
            m[side + str(s), hh] = send(
                source, rb.at[d, s - 1, hh], dev_zp if side == "P" else dev_zm
            )

        def total(hh):
            return ct[slot(0), hh].astype(F32) + rb[0, 3, hh].astype(F32) + rb[1, 3, hh].astype(F32)

        def exchange():
            for hh in range(2):
                m["P4", hh].wait_recv()
                m["M4", hh].wait_recv()
            xs[...] = total(1 - h).astype(BF16)
            m["H"] = send(xs, xr, dev_h)

        def finish():
            m["H"].wait_recv()
            return total(h) + xr[...].astype(F32)

        steps.append(first)
        steps.extend(functools.partial(part, j) for j in range(1, NZ))
        steps.extend(
            functools.partial(forward, side, s, hh)
            for s in (2, 3, 4) for side in "PM" for hh in range(2)
        )
        steps.append(exchange)
        return finish

    def reduce_hidden(steps):
        m = {}
        ca, cb = pl.ds(0, HR_A), pl.ds(HR_A, HR_B)
        cb1, cb2 = pl.ds(HR_A, HR_B1), pl.ds(HR_A + HR_B1, HR_B - HR_B1)
        p = part_h

        def at(x_, y_):
            return x_ * NY + y_

        def add(d, cols, value):
            p[d, :, cols] = (p[d, :, cols].astype(F32) + value.astype(F32)).astype(BF16)

        def hr0x():
            for i, y_ in enumerate((y2, yp, ym, y)):
                m["HX0", i] = send(p.at[at(xp, y_), :, cb], rx_b.at[i], dev_x)

        def hr0():
            m["HP0"] = send(p.at[at(x, y2), :, ca], r2_a.at[0], dev_yp)
            m["HM0"] = send(p.at[at(xp, y2), :, ca], r2_a.at[1], dev_ym)
            m["HP2b"] = send(p.at[at(xp, yp), :, ca], ry_a.at[0, 1], dev_yp)

        def hr1():
            m["HX0", 0].wait_recv()
            add(at(x, y2), cb, rx_b[0])
            m["HP1"] = send(p.at[at(x, y2), :, cb1], r2_b1, dev_yp)
            m["HM1"] = send(p.at[at(x, y2), :, cb2], r2_b2, dev_ym)

        def hr2m():
            m["HM0"].wait_recv()
            add(at(xp, ym), ca, r2_a[1])
            m["HM2b"] = send(p.at[at(xp, ym), :, ca], ry_a.at[1, 1], dev_ym)
            m["HM2a"] = send(p.at[at(x, ym), :, ca], ry_a.at[1, 0], dev_ym)

        def hr2p():
            m["HP0"].wait_recv()
            add(at(x, yp), ca, r2_a[0])
            m["HP2a"] = send(p.at[at(x, yp), :, ca], ry_a.at[0, 0], dev_yp)

        def hr3p():
            m["HX0", 1].wait_recv()
            add(at(x, yp), cb, rx_b[1])
            m["HP1"].wait_recv()
            add(at(x, yp), cb1, r2_b1[...])
            m["HP3"] = send(p.at[at(x, yp), :, cb], ry_b.at[0], dev_yp)

        def hr3m():
            m["HX0", 2].wait_recv()
            add(at(x, ym), cb, rx_b[2])
            m["HM1"].wait_recv()
            add(at(x, ym), cb2, r2_b2[...])
            m["HM3"] = send(p.at[at(x, ym), :, cb], ry_b.at[1], dev_ym)

        def hr4():
            m["HP2b"].wait_recv()
            m["HM2b"].wait_recv()
            d = at(xp, y)
            hs_a[...] = (
                p[d, :, ca].astype(F32) + ry_a[0, 1].astype(F32) + ry_a[1, 1].astype(F32)
            ).astype(BF16)
            m["HX1"] = send(hs_a, rx_a, dev_x)

        def hr5b():
            d = at(x, y)
            m["HX0", 3].wait_recv()
            m["HP3"].wait_recv()
            m["HM3"].wait_recv()
            hidden_out[:, cb] = (
                (p[d, :, cb].astype(F32) + rx_b[3].astype(F32))
                + (ry_b[0].astype(F32) + ry_b[1].astype(F32))
            ).astype(BF16)

        def hr5a():
            d = at(x, y)
            for name in ("HP2a", "HM2a", "HX1"):
                m[name].wait_recv()
            hidden_out[:, ca] = (
                (p[d, :, ca].astype(F32) + ry_a[0, 0].astype(F32))
                + (ry_a[1, 0].astype(F32) + rx_a[...].astype(F32))
            ).astype(BF16)

        steps.extend((hr0x, hr0, hr1, hr2m, hr2p, hr3p, hr3m, hr4, hr5b, hr5a))

    def rotate_all():
        key = (1 - c).astype(F32)
        order = lax.broadcasted_iota(jnp.int32, (HD // 2, 2 * TOK), 0).astype(F32)
        inverse = jnp.exp(order * F32(-LOG_BASE * 2.0 / HD))

        def body(d, carry):
            rows = pl.ds(pl.multiple_of(d * 2 * TOK, 2 * TOK), 2 * TOK)
            angles = inverse * pos_v[pl.ds(d, 1), :].astype(F32)
            cs, sn = jnp.cos(angles), jnp.sin(angles)
            cs = jnp.concatenate([cs, cs], axis=0).T
            sn = jnp.concatenate([sn, -sn], axis=0).T
            for head in range(QW // HD):
                cols = pl.ds(head * HD, HD)
                g = q_in[rows, cols].astype(F32)
                turned = g * cs + pltpu.roll(g, HD // 2, 1) * sn
                grads[d, :, :, cols] = turned.astype(BF16).reshape(2, TOK, HD)
            g = kv_own[rows, :].astype(F32) + kv_other[rows, :].astype(F32)
            cs, sn = cs * key + (1.0 - key), sn * key
            turned = g * cs + pltpu.roll(g, HD // 2, 1) * sn
            grads[d, :, :, pl.ds(QW, HD)] = turned.astype(BF16).reshape(2, TOK, HD)
            return carry

        lax.fori_loop(0, REP // (2 * TOK), body, 0)

    def transpose_all():
        def body(d, carry):
            cols = pl.ds(pl.multiple_of(d * 2 * TOK, 2 * TOK), 2 * TOK)
            grads_t[:, cols] = grads[d].reshape(2 * TOK, ROWS).T
            attn_t[:, cols] = attn_v[cols, :].T
            return carry

        lax.fori_loop(0, REP // (2 * TOK), body, 0)

    def hidden_partials(first, last):
        step = 512

        def body(i, carry):
            cols = pl.ds(pl.multiple_of(i * step, step), step)
            total = lax.dot_general(
                h_grads[...].reshape(REP // 2, 2 * ROWS), w_cat[cols, :],
                (((1,), (1,)), ((), ())), preferred_element_type=F32,
            )
            part_h[:, :, cols] = total.astype(BF16).reshape(2 * NY, TOK, step)
            return carry

        lax.fori_loop(first, last, body, 0)

    barrier = pltpu.get_barrier_semaphore()
    signal(barrier, dev_x, dev_yp, dev_ym, dev_c)
    pl.when(z % 2 == 0)(lambda: signal(barrier, dev_zp, dev_zm))
    pl.when(h == 0)(lambda: signal(barrier, dev_h))
    own_norm, own_out, held = [], [], {}
    load_own(normed, g_norm, own_norm, 0, SLOTS // 2)

    def reach_dp():
        pl.when(z % 2 == 0)(lambda: pl.semaphore_wait(ready_z, 2))
        pl.when(h == 0)(lambda: pl.semaphore_wait(ready_h, 1))

    steps = []
    for n, g, own in ((1, g_norm, own_norm), (2, g_out, own_out)):
        for phase in PHASES[n]:
            gather(g, own, phase, steps)
    finish_1 = reduce_dp(grads_t, g_norm, ct_q, sb_q, rb_q, xs_q, xr_q, steps, reach_dp)
    finish_2 = reduce_dp(attn_t, g_out, ct_o, sb_o, rb_o, xs_o, xr_o, steps, lambda: None)
    reduce_hidden(steps)
    def start():
        pl.semaphore_wait(barrier, 4 + 2 * (z % 2) + h)
        pl.when(z % 2 == 1)(lambda: signal(ready_z, dev_zp, dev_zm))
        pl.when(h == 1)(lambda: signal(ready_h, dev_h))

    def weights():
        held["lkv"] = load(d_keyvalue.at[:, pl.ds(pl.multiple_of(c * HD, HD), HD)], kv_own)
        held["kv"] = send(
            d_keyvalue.at[:, pl.ds(pl.multiple_of((1 - c) * HD, HD), HD)], kv_other, dev_c
        )
        held["lpos"] = load(positions, pos_v)
        held["lq"] = load(d_query, q_in)
        load_own(normed, g_norm, own_norm, SLOTS // 2, SLOTS)
        held["lattn"] = load(attn_out, attn_v)
        held["lwq"] = load(w_query, w_cat.at[:, pl.ds(0, QW)])
        held["lwkv"] = load(w_keyvalue, w_cat.at[:, pl.ds(QW, HD)])
        held["wq"] = send(w_query, w_cat.at[:, pl.ds(ROWS, QW)], dev_c)
        held["wkv"] = send(w_keyvalue, w_cat.at[:, pl.ds(ROWS + QW, HD)], dev_c)
        load_own(out_grad, g_out, own_out, 0, SLOTS)

    def rotate():
        for name in ("lpos", "lq", "lkv"):
            held[name].wait()
        held["kv"].wait_recv()
        rotate_all()
        held["g"] = send(grads.at[:, 1 - c], h_grads.at[:, :, pl.ds(ROWS, ROWS)], dev_c)
        held["lg"] = load(grads.at[:, c], h_grads.at[:, :, pl.ds(0, ROWS)])

    def transpose():
        held["lattn"].wait()
        transpose_all()

    def hidden(i):
        if i == 0:
            for name in ("lwq", "lwkv", "lg"):
                held[name].wait()
            for name in ("wq", "wkv", "g"):
                held[name].wait_recv()
        hidden_partials(2 * i, 2 * i + 2)

    def finish_q():
        total = finish_1()
        query_out[...] = total[:QW].T.astype(BF16)
        keyvalue_out[...] = total[QW:].T.astype(BF16)

    def finish_o():
        out_out[...] = finish_2().astype(BF16)

    steps.extend((start, weights, rotate, transpose))
    steps.extend(functools.partial(hidden, i) for i in range(4))
    steps.extend((finish_q, finish_o))
    assert sorted(PLAN) == list(range(len(steps)))
    issued = []
    waited = 0
    for at in PLAN:
        steps[at]()
        issued.append(len(messages))
        if len(issued) > LAG:
            for message in messages[waited:issued[-1 - LAG]]:
                message.wait_send()
            waited = issued[-1 - LAG]
    for message in messages[waited:]:
        message.wait_send()


def place(*refs):
    for i in range(4):
        refs[4 + i][...] = refs[i][...]


def local(normed, out_grad, attn_out, d_query, d_keyvalue, positions, w_query, w_keyvalue):
    vmem = pltpu.VMEM
    shapes = (
        jax.ShapeDtypeStruct((TOK, D), BF16),
        jax.ShapeDtypeStruct((BLK, QW), BF16),
        jax.ShapeDtypeStruct((BLK, HD), BF16),
        jax.ShapeDtypeStruct((QW, BLK), BF16),
    )
    results = pl.pallas_call(
        kernel,
        out_shape=tuple(vmem(shape.shape, shape.dtype) for shape in shapes),
        in_specs=[pl.BlockSpec(memory_space=pl.ANY)] * 8,
        out_specs=[pl.BlockSpec(memory_space=vmem)] * 4,
        scratch_shapes=[
            vmem((SLOTS, REP, BLK), BF16),
            vmem((SLOTS, REP, BLK), BF16),
            vmem((D, 2 * ROWS), BF16),
            vmem((2 * NY, 2, TOK, ROWS), BF16),
            vmem((2 * NY, TOK, 2 * ROWS), BF16),
            vmem((ROWS, REP), BF16),
            vmem((REP, QW), BF16),
            vmem((QW, REP), BF16),
            vmem((REP, QW), BF16),
            vmem((REP, HD), BF16),
            vmem((REP, HD), BF16),
            vmem((8, REP // 8), jnp.int32),
            vmem((2 * NY, TOK, D), BF16),
            vmem((NY, TOK, HR_B), BF16),
            vmem((2, TOK, HR_A), BF16),
            vmem((TOK, HR_B1), BF16),
            vmem((TOK, HR_B - HR_B1), BF16),
            vmem((2, 2, TOK, HR_A), BF16),
            vmem((2, TOK, HR_B), BF16),
            vmem((TOK, HR_A), BF16),
            vmem((TOK, HR_A), BF16),
        ]
        + [
            shape
            for rows in (ROWS, QW)
            for shape in (
                vmem((7, 2, rows, BLK), BF16),
                vmem((2, rows, BLK), BF16),
                vmem((2, 4, 2, rows, BLK), BF16),
                vmem((rows, BLK), BF16),
                vmem((rows, BLK), BF16),
            )
        ]
        + [
            pltpu.SemaphoreType.DMA((SEMS,)),
            pltpu.SemaphoreType.DMA((SEMS,)),
            pltpu.SemaphoreType.DMA((LOCAL_SEMS,)),
            pltpu.SemaphoreType.REGULAR,
            pltpu.SemaphoreType.REGULAR,
        ],
        compiler_params=pltpu.CompilerParams(
            collective_id=0, has_side_effects=True, vmem_limit_bytes=60 * 1024 * 1024
        ),
    )(
        normed, out_grad, attn_out, d_query, d_keyvalue, positions.reshape(8, REP // 8),
        w_query, w_keyvalue,
    )
    return pl.pallas_call(
        place,
        out_shape=shapes,
        in_specs=[pl.BlockSpec(memory_space=vmem)] * 4,
        out_specs=[pl.BlockSpec(memory_space=vmem)] * 4,
    )(*(pltpu.with_memory_space_constraint(result, vmem) for result in results))


def solution(mesh):
    return jax.shard_map(
        local,
        mesh=mesh,
        in_specs=(
            P(("dp", "tensor"), None),
            P(("dp", "tensor"), None),
            P("dp", "tensor"),
            P("dp", "tensor"),
            P("dp", "tensor"),
            P("dp"),
            P(None, "tensor"),
            P(None, "tensor"),
        ),
        out_specs=(
            P(("dp", "tensor"), None),
            P("dp", "tensor"),
            P("dp", "tensor"),
            P("tensor", "dp"),
        ),
        check_vma=False,
    )
```
